256 devices in a mesh: seq: 32 (over y, z_hi, core), head: 8 (over z_lo, x).
Axes of the slice: x: 4, y: 4, z: 8 (z_hi: 4, z_lo: 2; z = z_hi * 2 + z_lo), core: 2. Of those that a mesh axis runs over, the one named last changes fastest.
Arguments:
- queries: bfloat16 [8192, 3072], P('seq', 'head'), may hold values from -8 to 8
- keys: bfloat16 [8192, 3072], P('seq', 'head'), may hold values from -8 to 8
- values: bfloat16 [8192, 3072], P('seq', 'head'), may hold values from -6 to 6
- layer_grad: bfloat16 [8192, 3072], P('seq', 'head'), may hold values from -6 to 6
- out_weight: bfloat16 [3072, 3072], P('head'), may hold values from -0.109375 to 0.109375
- text_keys: bfloat16 [256, 3072], P(None, 'head'), may hold values from -6 to 6
- text_values: bfloat16 [256, 3072], P(None, 'head'), may hold values from -6 to 6
- extents: int32 [24, 3], P('head'), may hold values from 0 to 2, as said below
- text_mask: int32 [256], replicated, may hold values 0 or 1
Outputs:
- query_gradient: bfloat16 [8192, 3072], P('seq', 'head')
- key_grad: float32 [8192, 3072], P('seq', 'head')
- value_grad: float32 [8192, 3072], P('seq', 'head')
- text_key_grad: float32 [256, 3072], P('seq', 'head')
- text_value_gradient: float32 [256, 3072], P('seq', 'head')
The draws below stay inside these ranges and needn't reach their ends.
Inputs may be any that keep to these rules, and one draw needn't show every extreme that they name: `extents`: the time and height reach are 0 or 1, the width reach 0 to 2.
All inputs are finite; a program needn't handle non-finite values.
Results may differ from the reference program's by a relative error of at most 0.0066.
Values may be sent and summed in bfloat16 or wider, within the bound.
No kernel may reach another device: no remote copies, remote signals or barrier semaphores. Data moves between devices by JAX's collectives and lax.ppermute only.
A program may use at most 128 MiB of HBM per device.

```python
import jax
import jax.numpy as jnp
from jax import lax

HEADS = 24
DH = 128
MODEL_WIDTH = 3072
TT = 2
TH = 8
TW = 8
HT = 4
TEXT_TOKENS = 256
VID_DEV = 256
VIDEO = 8192
N_SEQ = 32


def draw_queries(key, part):
    key = jax.random.fold_in(key, 11)
    result = jnp.clip(jax.random.normal(key, (VIDEO, MODEL_WIDTH), jnp.float32), -8.0, 8.0)
    return result.astype(jnp.bfloat16)


def draw_keys(key, part):
    key = jax.random.fold_in(key, 13)
    result = jnp.clip(jax.random.normal(key, (VIDEO, MODEL_WIDTH), jnp.float32), -8.0, 8.0)
    return result.astype(jnp.bfloat16)


def draw_extents(key, part):
    key = jax.random.fold_in(key, 5)
    near_reach = jax.random.randint(key, (HEADS, 2), 0, 2, jnp.int32)
    wide_reach = jax.random.randint(jax.random.fold_in(key, 1), (HEADS, 1), 0, 3, jnp.int32)
    first_head = (jnp.arange(HEADS, dtype=jnp.int32) == 0)[:, None]
    near_reach = jnp.where(first_head, jnp.int32(1), near_reach)
    wide_reach = jnp.where(first_head, jnp.int32(2), wide_reach)
    return jnp.concatenate([near_reach, wide_reach], 1)


def touch_ends(values, own_key, least, top_value):
    longest = values.shape.index(max(values.shape))
    spots = []
    for shift in (0, 1):
        where = [jax.random.randint(jax.random.fold_in(own_key, axis), (), 0, length) for axis, length in enumerate(values.shape)]
        where[longest] = (where[longest] + shift) % values.shape[longest]
        spots.append(tuple(where))
    return values.at[spots[0]].set(least).at[spots[1]].set(top_value)


def level_of(stream_key, shape, split, low, top_value):
    gain, own = 1.0, jax.random.fold_in(stream_key, 6)
    for dim, parts in split:
        heights = jnp.exp(jax.random.uniform(jax.random.fold_in(own, dim), (parts,), jnp.float32, low / len(split), top_value / len(split)))
        gain = gain * jnp.repeat(heights, shape[dim] // parts).reshape([-1 if axis == dim else 1 for axis in range(len(shape))])
    return gain


def noise(rng, dims, scale, limit, split=(), kind=jnp.bfloat16):
    level = level_of(rng, dims, split, -0.22, 0.18) if split else 1.0
    values = jax.random.normal(rng, dims, jnp.float32) * scale * level
    return jnp.minimum(jnp.maximum(values, -limit), limit).astype(kind)


def setup_inputs(seed: int = 0) -> dict:
    arg_keys = jax.random.split(jax.random.key(seed), 10)
    queries = draw_queries(jax.random.fold_in(arg_keys[9], 71), 0)
    keys = draw_keys(jax.random.fold_in(arg_keys[9], 71), 0)
    values = noise(arg_keys[2], (VIDEO, MODEL_WIDTH), 1.0, 6.0, ((0, 32), (1, 8)))
    layer_grad = noise(arg_keys[3], (VIDEO, MODEL_WIDTH), 1.0, 6.0, ((0, 32), (1, 8)))
    out_weight = noise(arg_keys[4], (MODEL_WIDTH, MODEL_WIDTH), MODEL_WIDTH ** -0.5, 0.109375, ((0, 8),))
    text_keys = noise(arg_keys[5], (TEXT_TOKENS, MODEL_WIDTH), 1.0, 6.0, ((1, 8),))
    text_values = noise(arg_keys[6], (TEXT_TOKENS, MODEL_WIDTH), 1.0, 6.0, ((1, 8),))
    extents = draw_extents(jax.random.fold_in(arg_keys[9], 71), 0)
    text_mask = touch_ends((jax.random.randint(arg_keys[8], (TEXT_TOKENS,), 0, 4) < 3).astype(jnp.int32), jax.random.fold_in(arg_keys[8], 1), 0, 1)
    return {"queries": queries, "keys": keys, "values": values, "layer_grad": layer_grad, "out_weight": out_weight, "text_keys": text_keys, "text_values": text_values, "extents": extents, "text_mask": text_mask}


def window_mask(ext_one, row_index, n_rows, tokens):
    tile_size = TT * TH * TW
    tile_index = jnp.arange(tokens, dtype=jnp.int32) // tile_size
    time_off = jnp.array([-1, -1, -1, 0, 0, 0, 1, 1, 1], jnp.int32)
    height_off = jnp.array([-1, 0, 1, -1, 0, 1, -1, 0, 1], jnp.int32)
    n_time = n_rows // HT
    time_at = row_index // HT + time_off
    height_at = row_index % HT + height_off
    inside = (time_at >= 0) & (time_at < n_time) & (height_at >= 0) & (height_at < HT)
    near_block = inside & (jnp.abs(time_off) <= ext_one[0]) & (jnp.abs(height_off) <= ext_one[1])
    near_width = jnp.abs(tile_index[None, :] - tile_index[:, None]) <= ext_one[2]
    allowed = near_block[None, :, None] & near_width[:, None, :]
    return allowed.reshape(tokens, 9 * tokens)


def reference(queries, keys, values, layer_grad, out_weight, text_keys, text_values, extents, text_mask):
    highest = lax.Precision.HIGHEST
    inv_root = DH ** -0.5
    attn_grad = jnp.dot(layer_grad, out_weight.T, preferred_element_type=jnp.float32).astype(jnp.bfloat16)
    n_rows = N_SEQ
    tokens = VID_DEV
    margin = HT + 1

    def rows_of(array):
        return array.astype(jnp.float32).reshape(n_rows, tokens, HEADS, DH)

    query_rows = rows_of(queries)
    grad_rows = rows_of(attn_grad)
    padding = ((margin, margin), (0, 0), (0, 0), (0, 0))
    key_pad = jnp.pad(rows_of(keys), padding)
    value_pad = jnp.pad(rows_of(values), padding)
    text_key = text_keys.astype(jnp.float32).reshape(TEXT_TOKENS, HEADS, DH)
    text_value = text_values.astype(jnp.float32).reshape(TEXT_TOKENS, HEADS, DH)
    text_on = text_mask == 1
    video_tokens = 9 * tokens

    def neighbours(padded, row_index):
        blocks = [lax.dynamic_slice_in_dim(padded, row_index + margin + time_off * HT - 1, 3, 0) for time_off in (-1, 0, 1)]
        return jnp.concatenate(blocks, 0).reshape(video_tokens, HEADS, DH)

    def one_row(state_running, row_index):
        key_gradient_total, value_gradient_total, text_key_running, text_value_running = state_running
        query_here = query_rows[row_index]
        grad_here = grad_rows[row_index]
        near_key = jnp.concatenate([neighbours(key_pad, row_index), text_key], 0)
        near_value = jnp.concatenate([neighbours(value_pad, row_index), text_value], 0)
        video_allowed = jax.vmap(lambda ext_one: window_mask(ext_one, row_index, n_rows, tokens))(extents)
        allowed = jnp.concatenate([video_allowed,
                                   jnp.broadcast_to(text_on[None, None, :], (HEADS, tokens, TEXT_TOKENS))], 2)
        scores = jnp.einsum('qhd,khd->hqk', query_here, near_key, precision=highest) * inv_root
        scores = jnp.where(allowed, scores, -jnp.inf)
        row_max = jnp.max(scores, -1, keepdims=True)
        weights = jnp.where(allowed, jnp.exp(scores - row_max), jnp.float32(0.0))
        probs = weights / jnp.sum(weights, -1, keepdims=True)
        probs_b = lax.optimization_barrier(probs.astype(jnp.bfloat16)).astype(jnp.float32)
        dprobs = jnp.einsum('qhd,khd->hqk', grad_here, near_value, precision=highest)
        delta = jnp.sum(probs * dprobs, -1, keepdims=True)
        dscores = lax.optimization_barrier((probs * (dprobs - delta)).astype(jnp.bfloat16)).astype(jnp.float32)
        query_gradient = jnp.einsum('hqk,khd->qhd', dscores, near_key, precision=highest) * inv_root
        key_part = jnp.einsum('hqk,qhd->khd', dscores, query_here, precision=highest) * inv_root
        value_portion = jnp.einsum('hqk,qhd->khd', probs_b, grad_here, precision=highest)
        key_blocks = key_part[:video_tokens].reshape(3, 3, tokens, HEADS, DH)
        value_blocks = value_portion[:video_tokens].reshape(3, 3, tokens, HEADS, DH)
        for which in range(3):
            first_row = row_index + margin + (which - 1) * HT - 1
            old_key = lax.dynamic_slice_in_dim(key_gradient_total, first_row, 3, 0)
            key_gradient_total = lax.dynamic_update_slice_in_dim(key_gradient_total, old_key + key_blocks[which], first_row, 0)
            old_value = lax.dynamic_slice_in_dim(value_gradient_total, first_row, 3, 0)
            value_gradient_total = lax.dynamic_update_slice_in_dim(value_gradient_total, old_value + value_blocks[which], first_row, 0)
        text_key_running = text_key_running + key_part[video_tokens:]
        text_value_running = text_value_running + value_portion[video_tokens:]
        return (key_gradient_total, value_gradient_total, text_key_running, text_value_running), query_gradient

    start_state = (jnp.zeros_like(key_pad), jnp.zeros_like(value_pad),
                   jnp.zeros((TEXT_TOKENS, HEADS, DH), jnp.float32), jnp.zeros((TEXT_TOKENS, HEADS, DH), jnp.float32))
    closing_state, query_grads = lax.scan(one_row, start_state, jnp.arange(n_rows, dtype=jnp.int32))
    key_gradient_total, value_gradient_total, text_key_running, text_value_running = closing_state
    query_gradient = query_grads.reshape(VIDEO, MODEL_WIDTH).astype(jnp.bfloat16)
    key_grad = key_gradient_total[margin:margin + n_rows].reshape(VIDEO, MODEL_WIDTH).astype(jnp.float32)
    value_grad = value_gradient_total[margin:margin + n_rows].reshape(VIDEO, MODEL_WIDTH).astype(jnp.float32)
    text_key_grad = text_key_running.reshape(TEXT_TOKENS, MODEL_WIDTH).astype(jnp.float32)
    text_value_gradient = text_value_running.reshape(TEXT_TOKENS, MODEL_WIDTH).astype(jnp.float32)
    return (query_gradient, key_grad, value_grad, text_key_grad, text_value_gradient)
```

```python
import functools
import math

import jax
import jax.numpy as jnp
from jax import lax
from jax.experimental import pallas as pl
from jax.experimental.pallas import tpu as pltpu
from jax.sharding import PartitionSpec as P

DH = 128
TOK = 256
TEXT = 256
ROWS = 4
SPAN = 3 * TOK
QALL = ROWS * TOK
MSG = 3 * TOK + 16
INV_ROOT = DH ** (-0.5)
LOG2E = math.log2(math.e)
F32 = jnp.float32
BF16 = jnp.bfloat16
ANY = pl.BlockSpec(memory_space=pl.ANY)
VMEM = pl.BlockSpec(memory_space=pltpu.VMEM)
SMEM = pl.BlockSpec(memory_space=pltpu.SMEM)


def params():
    return pltpu.CompilerParams(vmem_limit_bytes=40 * 1024 * 1024)


def sds(shape, dtype):
    return jax.ShapeDtypeStruct(shape, dtype)


def dot_nt(a, b):
    return lax.dot_general(a, b, (((1,), (1,)), ((), ())), preferred_element_type=F32)


def dot_nn(a, b):
    return lax.dot_general(a, b, (((1,), (0,)), ((), ())), preferred_element_type=F32)


def dot_tn(a, b):
    return lax.dot_general(a, b, (((0,), (0,)), ((), ())), preferred_element_type=F32)


def out_pairs(phase):
    pairs = []
    for y in range(4):
        for zt in range(2):
            for h in range(4):
                head = (h - phase) % 4
                if head < 3:
                    pairs.append((y * 8 + zt * 4 + h, y * 8 + head * 2 + zt))
    return pairs


def back_pairs(phase):
    return [(b, a) for a, b in out_pairs(phase)]


def core_pairs():
    return [(s, s ^ 1) for s in range(32) if (s // 2) % 4 < 3]


def time_pairs():
    pairs = []
    for s in range(32):
        y, z_hi, c = s // 8, (s // 2) % 4, s % 2
        if z_hi < 3:
            other = y + 1 if c else y - 1
            if 0 <= other < 4:
                pairs.append((s, other * 8 + z_hi * 2 + 1 - c))
    return pairs


def head_pairs(dx, dz):
    return [(g, ((g // 4 + dz) % 2) * 4 + (g % 4 + dx) % 4) for g in range(8)]


def start_all(copies):
    for one in copies:
        one.start()


def wait_all(copies):
    for one in copies:
        one.wait()


def home_height():
    return lax.rem(lax.axis_index("seq"), 4)


def work_chip():
    return lax.rem(lax.div(lax.axis_index("seq"), 2), 4)


def pack_kernel(q_ref, k_ref, v_ref, o0, o1, o2, o3, sem):
    h = home_height()
    copies = []
    for phase, out in enumerate((o0, o1, o2, o3)):
        head = jnp.minimum(lax.rem(h - phase + 4, 4), 2)
        columns = pl.ds(pl.multiple_of(head * DH, DH), DH)
        for which, src in enumerate((q_ref, k_ref, v_ref)):
            copies.append(
                pltpu.make_async_copy(src.at[:, columns], out.at[which], sem.at[phase * 3 + which])
            )
    start_all(copies)
    wait_all(copies)


def project_kernel(c0, c1, c2, c3, c4, c5, c6, c7, w_ref, o0, o1, o2, o3):
    chunks = (c0, c1, c2, c3, c4, c5, c6, c7)
    g = lax.axis_index("head")
    h = home_height()
    gz, gx = lax.div(g, 4), lax.rem(g, 4)
    width = c0.shape[1]
    for phase, out in enumerate((o0, o1, o2, o3)):
        head = jnp.minimum(lax.rem(h - phase + 4, 4), 2)
        rows = pl.ds(pl.multiple_of(head * DH, DH), DH)
        total = None
        for which, chunk in enumerate(chunks):
            dz, dx = which // 4, which % 4
            src = lax.rem(gz + dz, 2) * 4 + lax.rem(gx - dx + 4, 4)
            columns = pl.ds(pl.multiple_of(src * width, width), width)
            term = dot_nt(chunk[...], w_ref[rows, columns])
            total = term if total is None else total + term
        out[...] = total.astype(BF16)


def window(ext_ref, chip):
    head = jnp.minimum(chip, 2)
    reach_t, reach_h, reach_w = ext_ref[head, 0], ext_ref[head, 1], ext_ref[head, 2]
    s = lax.axis_index("seq")
    y, c = lax.div(s, 8), lax.rem(s, 2)
    near = reach_t >= 1
    outside = ((y == 0) & (c == 0)) | ((y == 3) & (c == 1))
    return (True, near, near & jnp.logical_not(outside)), reach_h, reach_w >= 1


def span_bias(block_ok, reach_h, wide, key_h, first_h):
    lane = lax.broadcasted_iota(jnp.int32, (1, TOK), 1)
    left = lane < TOK // 2
    top, low = [], []
    for j in range(3):
        ok = jnp.abs(first_h + j - key_h) <= reach_h
        if block_ok is not True:
            ok = ok & block_ok
        same = jnp.where(ok, 0.0, -jnp.inf).astype(F32)
        cross = jnp.where(ok & wide, 0.0, -jnp.inf).astype(F32)
        top.append(jnp.where(left, same, cross))
        low.append(jnp.where(left, cross, same))
    return jnp.concatenate(top, 1), jnp.concatenate(low, 1)


def first_height(key_h):
    return jnp.clip(key_h - 1, 0, 1)


def fold(x, how):
    return how(x.reshape(x.shape[0] // 8, 8, x.shape[1]), 0)


def stats_kernel(
    ext_ref, m0, m1, m2, m3, core_kv, time_kv, tk_ref, tv_ref, tb_ref,
    lse_ref, mean_ref,
    kb, vb, qb, sb, st, run, sem,
):
    chip = work_chip()
    copies = []
    for phase, msg in enumerate((m0, m1, m2, m3)):
        h = lax.rem(chip + phase, 4)
        copies += [
            pltpu.make_async_copy(msg.at[0], qb.at[pl.ds(pl.multiple_of(h * TOK, TOK), TOK)], sem.at[phase * 7]),
            pltpu.make_async_copy(msg.at[1], kb.at[h], sem.at[phase * 7 + 1]),
            pltpu.make_async_copy(msg.at[2], vb.at[h], sem.at[phase * 7 + 2]),
            pltpu.make_async_copy(core_kv.at[phase, 0], kb.at[4 + h], sem.at[phase * 7 + 3]),
            pltpu.make_async_copy(core_kv.at[phase, 1], vb.at[4 + h], sem.at[phase * 7 + 4]),
            pltpu.make_async_copy(time_kv.at[phase, 0], kb.at[8 + h], sem.at[phase * 7 + 5]),
            pltpu.make_async_copy(time_kv.at[phase, 1], vb.at[8 + h], sem.at[phase * 7 + 6]),
        ]
    start_all(copies)
    wait_all(copies)
    block_ok, reach_h, wide = window(ext_ref, chip)
    head = jnp.minimum(chip, 2)
    columns = pl.ds(pl.multiple_of(head * DH, DH), DH)
    factor = INV_ROOT * LOG2E

    text = dot_nt(tk_ref[:, columns], qb[...]) * factor + tb_ref[...]
    st[...] = text
    run[...] = fold(text, jnp.max)

    for part in range(3):

        def first(key_h, carry, part=part):
            h0 = first_height(key_h)
            rows = pl.ds(pl.multiple_of(h0 * TOK, TOK), SPAN)
            top, low = span_bias(block_ok[part], reach_h, wide, key_h, h0)
            s = dot_nt(kb[part * 4 + key_h], qb[rows, :]) * factor
            a, b = s[: TOK // 2] + top, s[TOK // 2 :] + low
            sb[part * 4 + key_h, : TOK // 2] = a
            sb[part * 4 + key_h, TOK // 2 :] = b
            run[:, rows] = jnp.maximum(run[:, rows], jnp.maximum(fold(a, jnp.max), fold(b, jnp.max)))
            return carry

        lax.fori_loop(0, 4, first, 0)

    top_score = jnp.max(run[...], 0, keepdims=True)
    lse_ref[...] = top_score
    weights = jnp.exp2(st[...] - top_score)
    run[...] = fold(weights, jnp.sum)
    mean_ref[...] = dot_tn(tv_ref[:, columns], weights.astype(BF16))

    def second(block, carry):
        key_h = lax.rem(block, 4)
        rows = pl.ds(pl.multiple_of(first_height(key_h) * TOK, TOK), SPAN)
        weights = jnp.exp2(sb[block] - lse_ref[:, rows])
        run[:, rows] += fold(weights, jnp.sum)
        mean_ref[:, rows] += dot_tn(vb[block], weights.astype(BF16))
        return carry

    lax.fori_loop(0, 12, second, 0)
    total = jnp.sum(run[...], 0, keepdims=True)
    lse_ref[...] = top_score + jnp.log2(total)
    mean_ref[...] = mean_ref[...] / total


def block_terms(keys, values, query, grad, bias, delta, factor):
    s = dot_nt(keys, query) * factor
    if isinstance(bias, tuple):
        top, low = bias
        half = TOK // 2
        probs = jnp.concatenate([jnp.exp2(s[:half] + top), jnp.exp2(s[half:] + low)], 0)
    else:
        probs = jnp.exp2(s + bias)
    dprobs = dot_nt(values, grad)
    dscores = (probs * (dprobs - delta)).astype(BF16)
    return probs.astype(BF16), dscores


def grad_kernel(part, m_refs, g_refs, kv_ref, ext_ref, lse_ref, delta_ref, dq_in, out_ref, dq_out, kb, vb, qb, gb, sem):
    chip = work_chip()
    copies = []
    for phase in range(4):
        h = lax.rem(chip + phase, 4)
        rows = pl.ds(pl.multiple_of(h * TOK, TOK), TOK)
        msg = m_refs[phase]
        key_src = msg.at[1] if part == 0 else kv_ref.at[phase, 0]
        value_src = msg.at[2] if part == 0 else kv_ref.at[phase, 1]
        copies += [
            pltpu.make_async_copy(msg.at[0], qb.at[rows], sem.at[phase * 4]),
            pltpu.make_async_copy(g_refs[phase], gb.at[rows], sem.at[phase * 4 + 1]),
            pltpu.make_async_copy(key_src, kb.at[h], sem.at[phase * 4 + 2]),
            pltpu.make_async_copy(value_src, vb.at[h], sem.at[phase * 4 + 3]),
        ]
    start_all(copies)
    wait_all(copies)
    if dq_in is None:
        dq_out[...] = jnp.zeros_like(dq_out)
    else:
        dq_out[...] = dq_in[...]
    block_ok, reach_h, wide = window(ext_ref, chip)
    factor = INV_ROOT * LOG2E

    def body(key_h, carry):
        h0 = first_height(key_h)
        rows = pl.ds(pl.multiple_of(h0 * TOK, TOK), SPAN)
        top, low = span_bias(block_ok[part], reach_h, wide, key_h, h0)
        lse = lse_ref[:, rows]
        query, grad, keys = qb[rows, :], gb[rows, :], kb[key_h]
        probs, dscores = block_terms(
            keys, vb[key_h], query, grad, (top - lse, low - lse), delta_ref[:, rows], factor
        )
        out_ref[key_h, 0] = (dot_nn(dscores, query) * INV_ROOT).astype(out_ref.dtype)
        out_ref[key_h, 1] = dot_nn(probs, grad).astype(out_ref.dtype)
        dq_out[:, rows] += dot_tn(keys, dscores)
        return carry

    lax.fori_loop(0, 4, body, 0)


def time_grad_kernel(
    ext_ref, m0, m1, m2, m3, g0, g1, g2, g3, kv_ref, lse_ref, mean_ref, tk_ref, tv_ref, tb_ref,
    out_ref, dq_ref, delta_ref, text_ref,
    kb, vb, qb, gb, sem,
):
    chip = work_chip()
    copies = []
    for phase, src in enumerate((g0, g1, g2, g3)):
        h = lax.rem(chip + phase, 4)
        rows = pl.ds(pl.multiple_of(h * TOK, TOK), TOK)
        copies.append(pltpu.make_async_copy(src, gb.at[rows], sem.at[phase]))
    start_all(copies)
    wait_all(copies)
    delta_ref[...] = jnp.sum(gb[...].astype(F32).T * mean_ref[...], 0, keepdims=True)
    grad_kernel(
        2, (m0, m1, m2, m3), (g0, g1, g2, g3), kv_ref, ext_ref, lse_ref, delta_ref, None,
        out_ref, dq_ref, kb, vb, qb, gb, sem,
    )
    head = jnp.minimum(chip, 2)
    columns = pl.ds(pl.multiple_of(head * DH, DH), DH)
    keys = tk_ref[:, columns]
    probs, dscores = block_terms(
        keys, tv_ref[:, columns], qb[...], gb[...], tb_ref[...] - lse_ref[...], delta_ref[...],
        INV_ROOT * LOG2E,
    )
    dq_ref[...] += dot_tn(keys, dscores)
    text_ref[:, :DH] = (dot_nn(dscores, qb[...]) * INV_ROOT).astype(BF16)
    text_ref[:, DH:] = dot_nn(probs, gb[...]).astype(BF16)


def core_grad_kernel(
    ext_ref, m0, m1, m2, m3, g0, g1, g2, g3, kv_ref, lse_ref, delta_ref, dq_in,
    out_ref, dq_ref, kb, vb, qb, gb, sem,
):
    grad_kernel(
        1, (m0, m1, m2, m3), (g0, g1, g2, g3), kv_ref, ext_ref, lse_ref, delta_ref, dq_in,
        out_ref, dq_ref, kb, vb, qb, gb, sem,
    )


def own_grad_kernel(
    ext_ref, m0, m1, m2, m3, g0, g1, g2, g3, lse_ref, delta_ref, dq_in,
    out_ref, dq_final, dq_run, kb, vb, qb, gb, sem,
):
    grad_kernel(
        0, (m0, m1, m2, m3), (g0, g1, g2, g3), None, ext_ref, lse_ref, delta_ref, dq_in,
        out_ref, dq_run, kb, vb, qb, gb, sem,
    )
    for h in range(ROWS):
        dq_final[h] = (dq_run[:, h * TOK : (h + 1) * TOK].T * INV_ROOT).astype(BF16)


def combine_kernel(own, core, time, dq, text, o0, o1, o2, o3, text_sum):
    chip = work_chip()
    text_sum[...] = jnp.sum(text[...].astype(F32), 0)
    for phase, out in enumerate((o0, o1, o2, o3)):
        h = lax.rem(chip + phase, 4)
        out[:TOK] = dq[h]
        for which in range(2):
            total = own[h, which] + core[h, which].astype(F32) + time[h, which].astype(F32)
            out[(1 + which) * TOK : (2 + which) * TOK] = total.astype(BF16)
        share = text_sum[pl.ds(pl.multiple_of(h * 8, 8), 8), :]
        out[3 * TOK :] = jnp.concatenate([share[:, :DH], share[:, DH:]], 0).astype(BF16)


def unpack_kernel(r0, r1, r2, r3, dq, dk, dv, tk, tv, buf, sem):
    h = home_height()
    copies = []
    for phase, src in enumerate((r0, r1, r2, r3)):
        head = lax.rem(h - phase + 4, 4)
        copies.append(pltpu.make_async_copy(src, buf.at[head], sem.at[phase]))
    start_all(copies)
    wait_all(copies)
    for head in range(3):
        columns = slice(head * DH, (head + 1) * DH)
        dq[:, columns] = buf[head, :TOK]
        dk[:, columns] = buf[head, TOK : 2 * TOK].astype(F32)
        dv[:, columns] = buf[head, 2 * TOK : 3 * TOK].astype(F32)
        share = buf[head, 3 * TOK :].astype(F32)
        tk[:, columns] = share[:8]
        tv[:, columns] = share[8:]


def per_device(queries, keys, values, layer_grad, out_weight, text_keys, text_values, extents, text_mask):
    block = sds((TOK, DH), BF16)
    text_bias = jnp.where(text_mask == 1, 0.0, -jnp.inf).astype(F32)[:, None]

    packed = pl.pallas_call(
        pack_kernel,
        in_specs=[ANY] * 3,
        out_specs=[ANY] * 4,
        out_shape=[sds((3, TOK, DH), BF16)] * 4,
        scratch_shapes=[pltpu.SemaphoreType.DMA((12,))],
        compiler_params=params(),
        name="pack_heads",
    )(queries, keys, values)

    chunks = [
        layer_grad if which == 0 else lax.ppermute(layer_grad, "head", head_pairs(which % 4, which // 4))
        for which in range(8)
    ]
    msgs = [lax.ppermute(one, "seq", out_pairs(phase)) for phase, one in enumerate(packed)]
    kv = jnp.stack([one[1:] for one in msgs])
    core_kv = lax.ppermute(kv, "seq", core_pairs())
    time_kv = lax.ppermute(kv, "seq", time_pairs())

    grads = pl.pallas_call(
        project_kernel,
        in_specs=[VMEM] * 9,
        out_specs=[VMEM] * 4,
        out_shape=[block] * 4,
        compiler_params=params(),
        name="project",
    )(*chunks, out_weight)
    grads = [lax.ppermute(one, "seq", out_pairs(phase)) for phase, one in enumerate(grads)]

    flops_block = 2 * TOK * SPAN * DH
    lse, mean = pl.pallas_call(
        stats_kernel,
        in_specs=[SMEM] + [ANY] * 6 + [VMEM] * 3,
        out_specs=[VMEM] * 2,
        out_shape=[sds((1, QALL), F32), sds((DH, QALL), F32)],
        scratch_shapes=[
            pltpu.VMEM((12, TOK, DH), BF16),
            pltpu.VMEM((12, TOK, DH), BF16),
            pltpu.VMEM((QALL, DH), BF16),
            pltpu.VMEM((12, TOK, SPAN), F32),
            pltpu.VMEM((TEXT, QALL), F32),
            pltpu.VMEM((8, QALL), F32),
            pltpu.SemaphoreType.DMA((28,)),
        ],
        compiler_params=params(),
        cost_estimate=pl.CostEstimate(flops=26 * flops_block, bytes_accessed=3_000_000, transcendentals=12 * TOK * SPAN),
        name="softmax_stats",
    )(extents, *msgs, core_kv, time_kv, text_keys, text_values, text_bias)

    scratch = [
        pltpu.VMEM((4, TOK, DH), BF16),
        pltpu.VMEM((4, TOK, DH), BF16),
        pltpu.VMEM((QALL, DH), BF16),
        pltpu.VMEM((QALL, DH), BF16),
        pltpu.SemaphoreType.DMA((16,)),
    ]
    cost = pl.CostEstimate(flops=20 * flops_block, bytes_accessed=2_000_000, transcendentals=4 * TOK * SPAN)
    half_sum = sds((4, 2, TOK, DH), BF16)
    dq_run = sds((DH, QALL), F32)
    time_part, dq, delta, text_part = pl.pallas_call(
        time_grad_kernel,
        in_specs=[SMEM] + [ANY] * 9 + [VMEM] * 5,
        out_specs=[VMEM] * 4,
        out_shape=[half_sum, dq_run, sds((1, QALL), F32), sds((TEXT, 2 * DH), BF16)],
        scratch_shapes=scratch,
        compiler_params=params(),
        cost_estimate=cost,
        name="time_and_text_grads",
    )(extents, *msgs, *grads, time_kv, lse, mean, text_keys, text_values, text_bias)
    time_back = lax.ppermute(time_part, "seq", time_pairs())
    groups = [[y * 8 + z_hi * 2 + c for y in range(4) for c in range(2)] for z_hi in range(4)]
    text_back = lax.all_to_all(
        text_part.reshape(8, TEXT // 8, 2 * DH), "seq", 0, 0, axis_index_groups=groups
    )

    core_part, dq = pl.pallas_call(
        core_grad_kernel,
        in_specs=[SMEM] + [ANY] * 9 + [VMEM] * 3,
        out_specs=[VMEM] * 2,
        out_shape=[half_sum, dq_run],
        scratch_shapes=scratch,
        compiler_params=params(),
        cost_estimate=cost,
        name="core_grads",
    )(extents, *msgs, *grads, core_kv, lse, delta, dq)
    core_back = lax.ppermute(core_part, "seq", core_pairs())

    own_part, dq = pl.pallas_call(
        own_grad_kernel,
        in_specs=[SMEM] + [ANY] * 8 + [VMEM] * 3,
        out_specs=[VMEM] * 2,
        out_shape=[sds((4, 2, TOK, DH), F32), sds((4, TOK, DH), BF16)],
        scratch_shapes=[pltpu.VMEM((DH, QALL), F32)] + scratch,
        compiler_params=params(),
        cost_estimate=cost,
        name="own_grads",
    )(extents, *msgs, *grads, lse, delta, dq)

    results = pl.pallas_call(
        combine_kernel,
        in_specs=[VMEM] * 5,
        out_specs=[VMEM] * 4,
        out_shape=[sds((MSG, DH), BF16)] * 4,
        scratch_shapes=[pltpu.VMEM((TEXT // 8, 2 * DH), F32)],
        compiler_params=params(),
        name="combine",
    )(own_part, core_back, time_back, dq, text_back)
    results = [lax.ppermute(one, "seq", back_pairs(phase)) for phase, one in enumerate(results)]

    width = 3 * DH
    return pl.pallas_call(
        unpack_kernel,
        in_specs=[ANY] * 4,
        out_specs=[VMEM] * 5,
        out_shape=[
            sds((TOK, width), BF16),
            sds((TOK, width), F32),
            sds((TOK, width), F32),
            sds((8, width), F32),
            sds((8, width), F32),
        ],
        scratch_shapes=[pltpu.VMEM((4, MSG, DH), BF16), pltpu.SemaphoreType.DMA((4,))],
        compiler_params=params(),
        name="unpack",
    )(*results)


def solution(mesh):
    return jax.shard_map(
        per_device,
        mesh=mesh,
        in_specs=(
            P("seq", "head"),
            P("seq", "head"),
            P("seq", "head"),
            P("seq", "head"),
            P("head", None),
            P(None, "head"),
            P(None, "head"),
            P("head", None),
            P(),
        ),
        out_specs=(P("seq", "head"),) * 5,
        check_vma=False,
    )
```

```python
import functools
import math

import jax
import jax.numpy as jnp
from jax import lax
from jax.experimental import pallas as pl
from jax.experimental.pallas import tpu as pltpu
from jax.sharding import PartitionSpec as P

DH = 128
TOK = 256
TEXT = 256
ROWS = 4
SPAN = 3 * TOK
QALL = ROWS * TOK
MSG = 3 * TOK + 16
INV_ROOT = DH ** (-0.5)
LOG2E = math.log2(math.e)
F32 = jnp.float32
BF16 = jnp.bfloat16
ANY = pl.BlockSpec(memory_space=pltpu.HBM)
VMEM = pl.BlockSpec(memory_space=pltpu.VMEM)
SMEM = pl.BlockSpec(memory_space=pltpu.SMEM)


def params(mib=12):
    return pltpu.CompilerParams(vmem_limit_bytes=mib * 1024 * 1024)


def sds(shape, dtype):
    return jax.ShapeDtypeStruct(shape, dtype)


def dot_nt(a, b):
    return lax.dot_general(a, b, (((1,), (1,)), ((), ())), preferred_element_type=F32)


def dot_nn(a, b):
    return lax.dot_general(a, b, (((1,), (0,)), ((), ())), preferred_element_type=F32)


def dot_tn(a, b):
    return lax.dot_general(a, b, (((0,), (0,)), ((), ())), preferred_element_type=F32)


def sent_head(phase, h):
    far, swap = (1, 0, 1, 0)[phase], phase // 2
    return ((h >> 1) ^ far) + 2 * ((h & 1) ^ swap)


def received_height(phase, chip):
    far, swap = (1, 0, 1, 0)[phase], phase // 2
    return 2 * ((chip & 1) ^ far) + ((chip >> 1) ^ swap)


def out_pairs(phase):
    pairs = []
    for y in range(4):
        for zt in range(2):
            for h in range(4):
                head = sent_head(phase, h)
                if head < 3:
                    pairs.append((y * 8 + zt * 4 + h, y * 8 + head * 2 + zt))
    return pairs


def back_pairs(phase):
    return [(b, a) for a, b in out_pairs(phase)]


def core_pairs():
    return [(s, s ^ 1) for s in range(32) if (s // 2) % 4 < 3]


def time_pairs():
    pairs = []
    for s in range(32):
        y, z_hi, c = s // 8, (s // 2) % 4, s % 2
        if z_hi < 3:
            other = y + 1 if c else y - 1
            if 0 <= other < 4:
                pairs.append((s, other * 8 + z_hi * 2 + 1 - c))
    return pairs


def head_pairs(dx, dz):
    return [(g, ((g // 4 + dz) % 2) * 4 + (g % 4 + dx) % 4) for g in range(8)]


def start_all(copies):
    for one in copies:
        one.start()


def wait_all(copies):
    for one in copies:
        one.wait()


def home_height():
    return lax.axis_index("seq") & 3


def work_chip():
    return (lax.axis_index("seq") >> 1) & 3


def pack_kernel(q_ref, k_ref, v_ref, o0, o1, o2, o3, sem):
    h = home_height()
    copies = []
    for phase, out in enumerate((o0, o1, o2, o3)):
        head = jnp.minimum(sent_head(phase, h), 2)
        columns = pl.ds(pl.multiple_of(head * DH, DH), DH)
        for which, src in enumerate((q_ref, k_ref, v_ref)):
            copies.append(
                pltpu.make_async_copy(src.at[:, columns], out.at[which], sem.at[phase * 3 + which])
            )
    start_all(copies)
    wait_all(copies)


def project_kernel(c0, c1, c2, c3, c4, c5, c6, c7, w_ref, o0, o1, o2, o3):
    chunks = (c0, c1, c2, c3, c4, c5, c6, c7)
    g = lax.axis_index("head")
    h = home_height()
    gz, gx = lax.div(g, 4), lax.rem(g, 4)
    width = c0.shape[1]
    for phase, out in enumerate((o0, o1, o2, o3)):
        head = jnp.minimum(sent_head(phase, h), 2)
        rows = pl.ds(pl.multiple_of(head * DH, DH), DH)
        total = None
        for which, chunk in enumerate(chunks):
            dz, dx = which // 4, which % 4
            src = lax.rem(gz + dz, 2) * 4 + lax.rem(gx - dx + 4, 4)
            columns = pl.ds(pl.multiple_of(src * width, width), width)
            term = dot_nt(chunk[...], w_ref[rows, columns])
            total = term if total is None else total + term
        out[...] = total.astype(BF16)


def window(ext_ref, chip):
    head = jnp.minimum(chip, 2)
    reach_t, reach_h, reach_w = ext_ref[head, 0], ext_ref[head, 1], ext_ref[head, 2]
    s = lax.axis_index("seq")
    y, c = lax.div(s, 8), lax.rem(s, 2)
    near = reach_t >= 1
    outside = ((y == 0) & (c == 0)) | ((y == 3) & (c == 1))
    return (True, near, near & jnp.logical_not(outside)), reach_h, reach_w >= 1


def span_bias(block_ok, reach_h, wide, key_h, first_h):
    lane = lax.broadcasted_iota(jnp.int32, (1, TOK), 1)
    left = lane < TOK // 2
    top, low = [], []
    for j in range(3):
        ok = jnp.abs(first_h + j - key_h) <= reach_h
        if block_ok is not True:
            ok = ok & block_ok
        same = jnp.where(ok, 0.0, -jnp.inf).astype(F32)
        cross = jnp.where(ok & wide, 0.0, -jnp.inf).astype(F32)
        top.append(jnp.where(left, same, cross))
        low.append(jnp.where(left, cross, same))
    return jnp.concatenate(top, 1), jnp.concatenate(low, 1)


def first_height(key_h):
    return jnp.clip(key_h - 1, 0, 1)


def fold(x, how):
    return how(x.reshape(x.shape[0] // 8, 8, x.shape[1]), 0)


def stats_kernel(
    ext_ref, m0, m1, m2, m3, core_kv, time_kv, tk_ref, tv_ref, tb_ref,
    lse_ref, mean_ref,
    kb, vb, qb, sb, st, run,
):
    chip = work_chip()
    for phase, msg in enumerate((m0, m1, m2, m3)):
        h = received_height(phase, chip)
        qb[pl.ds(pl.multiple_of(h * TOK, TOK), TOK), :] = msg[0]
        kb[h], vb[h] = msg[1], msg[2]
        kb[4 + h], vb[4 + h] = core_kv[phase, 0], core_kv[phase, 1]
        kb[8 + h], vb[8 + h] = time_kv[phase, 0], time_kv[phase, 1]
    block_ok, reach_h, wide = window(ext_ref, chip)
    head = jnp.minimum(chip, 2)
    columns = pl.ds(pl.multiple_of(head * DH, DH), DH)
    factor = INV_ROOT * LOG2E

    text = dot_nt(tk_ref[:, columns], qb[...]) * factor + tb_ref[...]
    st[...] = text
    run[...] = fold(text, jnp.max)

    for part in range(3):

        def first(key_h, carry, part=part):
            h0 = first_height(key_h)
            rows = pl.ds(pl.multiple_of(h0 * TOK, TOK), SPAN)
            top, low = span_bias(block_ok[part], reach_h, wide, key_h, h0)
            s = dot_nt(kb[part * 4 + key_h], qb[rows, :]) * factor
            a, b = s[: TOK // 2] + top, s[TOK // 2 :] + low
            sb[part * 4 + key_h, : TOK // 2] = a
            sb[part * 4 + key_h, TOK // 2 :] = b
            run[:, rows] = jnp.maximum(run[:, rows], jnp.maximum(fold(a, jnp.max), fold(b, jnp.max)))
            return carry

        lax.fori_loop(0, 4, first, 0, unroll=True)

    top_score = jnp.max(run[...], 0, keepdims=True)
    lse_ref[...] = top_score
    weights = jnp.exp2(st[...] - top_score)
    run[...] = fold(weights, jnp.sum)
    mean_ref[...] = dot_tn(tv_ref[:, columns], weights.astype(BF16))

    def second(block, carry):
        key_h = lax.rem(block, 4)
        rows = pl.ds(pl.multiple_of(first_height(key_h) * TOK, TOK), SPAN)
        weights = jnp.exp2(sb[block] - lse_ref[:, rows])
        run[:, rows] += fold(weights, jnp.sum)
        mean_ref[:, rows] += dot_tn(vb[block], weights.astype(BF16))
        return carry

    lax.fori_loop(0, 12, second, 0, unroll=4)
    total = jnp.sum(run[...], 0, keepdims=True)
    lse_ref[...] = top_score + jnp.log2(total)
    mean_ref[...] = mean_ref[...] / total


def block_terms(keys, values, query, grad, bias, delta, factor):
    s = dot_nt(keys, query) * factor
    if isinstance(bias, tuple):
        top, low = bias
        half = TOK // 2
        probs = jnp.concatenate([jnp.exp2(s[:half] + top), jnp.exp2(s[half:] + low)], 0)
    else:
        probs = jnp.exp2(s + bias)
    dprobs = dot_nt(values, grad)
    dscores = (probs * (dprobs - delta)).astype(BF16)
    return probs.astype(BF16), dscores


def place_rows(chip, refs, out):
    for phase, ref in enumerate(refs):
        rows = pl.ds(pl.multiple_of(received_height(phase, chip) * TOK, TOK), TOK)
        out[rows, :] = ref[...]


def part_grads(part, m_refs, kv_ref, ext_ref, lse_ref, delta_ref, out_ref, dq_ref, kb, vb, qb, gb):
    chip = work_chip()
    for phase in range(4):
        h = received_height(phase, chip)
        kb[h] = m_refs[phase][1] if part == 0 else kv_ref[phase, 0]
        vb[h] = m_refs[phase][2] if part == 0 else kv_ref[phase, 1]
    block_ok, reach_h, wide = window(ext_ref, chip)
    factor = INV_ROOT * LOG2E

    def body(key_h, carry):
        h0 = first_height(key_h)
        rows = pl.ds(pl.multiple_of(h0 * TOK, TOK), SPAN)
        top, low = span_bias(block_ok[part], reach_h, wide, key_h, h0)
        lse = lse_ref[:, rows]
        query, grad, keys = qb[rows, :], gb[rows, :], kb[key_h]
        probs, dscores = block_terms(
            keys, vb[key_h], query, grad, (top - lse, low - lse), delta_ref[:, rows], factor
        )
        out_ref[key_h, 0] = (dot_nn(dscores, query) * INV_ROOT).astype(out_ref.dtype)
        out_ref[key_h, 1] = dot_nn(probs, grad).astype(out_ref.dtype)
        dq_ref[:, rows] += dot_tn(keys, dscores)
        return carry

    lax.fori_loop(0, 4, body, 0, unroll=True)


def time_grads_kernel(
    ext_ref, m0, m1, m2, m3, g0, g1, g2, g3, time_kv, lse_ref, mean_ref, tk_ref, tv_ref, tb_ref,
    time_out, text_ref, dq_ref, delta_ref, gb,
    kb, vb, qb,
):
    chip = work_chip()
    m_refs = (m0, m1, m2, m3)
    place_rows(chip, [ref.at[0] for ref in m_refs], qb)
    place_rows(chip, (g0, g1, g2, g3), gb)
    delta_ref[...] = jnp.sum(gb[...].astype(F32).T * mean_ref[...], 0, keepdims=True)
    head = jnp.minimum(chip, 2)
    columns = pl.ds(pl.multiple_of(head * DH, DH), DH)
    keys = tk_ref[:, columns]
    probs, dscores = block_terms(
        keys, tv_ref[:, columns], qb[...], gb[...], tb_ref[...] - lse_ref[...], delta_ref[...],
        INV_ROOT * LOG2E,
    )
    dq_ref[...] = dot_tn(keys, dscores)
    text_ref[:, :DH] = (dot_nn(dscores, qb[...]) * INV_ROOT).astype(BF16)
    text_ref[:, DH:] = dot_nn(probs, gb[...]).astype(BF16)
    part_grads(2, m_refs, time_kv, ext_ref, lse_ref, delta_ref, time_out, dq_ref, kb, vb, qb, gb)


def near_grads_kernel(
    ext_ref, m0, m1, m2, m3, core_kv, lse_ref, dq_in, delta_ref, gb,
    core_out, own_out,
    kb, vb, qb, dq_run,
):
    m_refs = (m0, m1, m2, m3)
    place_rows(work_chip(), [ref.at[0] for ref in m_refs], qb)
    dq_run[...] = dq_in[...]
    part_grads(1, m_refs, core_kv, ext_ref, lse_ref, delta_ref, core_out, dq_run, kb, vb, qb, gb)
    part_grads(0, m_refs, None, ext_ref, lse_ref, delta_ref, own_out, dq_run, kb, vb, qb, gb)
    for h in range(ROWS):
        own_out[h, 2] = dq_run[:, h * TOK : (h + 1) * TOK].T * INV_ROOT


def combine_kernel(own, core, time, text, o0, o1, o2, o3, text_sum):
    chip = work_chip()
    text_sum[...] = jnp.sum(text[...].astype(F32), 0)
    for phase, out in enumerate((o0, o1, o2, o3)):
        h = received_height(phase, chip)
        out[:TOK] = own[h, 2].astype(BF16)
        for which in range(2):
            total = own[h, which] + core[h, which].astype(F32) + time[h, which].astype(F32)
            out[(1 + which) * TOK : (2 + which) * TOK] = total.astype(BF16)
        share = text_sum[pl.ds(pl.multiple_of(h * 8, 8), 8), :]
        out[3 * TOK :] = jnp.concatenate([share[:, :DH], share[:, DH:]], 0).astype(BF16)


def unpack_kernel(r0, r1, r2, r3, dq, dk, dv, tk, tv, buf):
    h = home_height()
    for phase, src in enumerate((r0, r1, r2, r3)):
        buf[sent_head(phase, h)] = src[...]
    for head in range(3):
        columns = slice(head * DH, (head + 1) * DH)
        dq[:, columns] = buf[head, :TOK]
        dk[:, columns] = buf[head, TOK : 2 * TOK].astype(F32)
        dv[:, columns] = buf[head, 2 * TOK : 3 * TOK].astype(F32)
        share = buf[head, 3 * TOK :].astype(F32)
        tk[:, columns] = share[:8]
        tv[:, columns] = share[8:]


def per_device(queries, keys, values, layer_grad, out_weight, text_keys, text_values, extents, text_mask):
    block = sds((TOK, DH), BF16)
    text_bias = jnp.where(text_mask == 1, 0.0, -jnp.inf).astype(F32)[:, None]

    packed = pl.pallas_call(
        pack_kernel,
        in_specs=[ANY] * 3,
        out_specs=[ANY] * 4,
        out_shape=[sds((3, TOK, DH), BF16)] * 4,
        scratch_shapes=[pltpu.SemaphoreType.DMA((12,))],
        compiler_params=params(),
        name="pack_heads",
    )(queries, keys, values)

    beside = lax.ppermute(layer_grad, "head", head_pairs(0, 1))
    chunks = [
        src if dx == 0 else lax.ppermute(src, "head", head_pairs(dx, 0))
        for src in (layer_grad, beside)
        for dx in range(4)
    ]
    packed = list(packed)
    packed[1:], chunks[1] = lax.optimization_barrier((packed[1:], chunks[1]))
    msgs = [lax.ppermute(one, "seq", out_pairs(phase)) for phase, one in enumerate(packed)]
    msgs, chunks = lax.optimization_barrier((msgs, chunks))
    kv = jnp.stack([one[1:] for one in msgs])
    core_kv = lax.ppermute(kv, "seq", core_pairs())
    time_kv = lax.ppermute(kv, "seq", time_pairs())

    grads = pl.pallas_call(
        project_kernel,
        in_specs=[VMEM] * 9,
        out_specs=[VMEM] * 4,
        out_shape=[block] * 4,
        compiler_params=params(),
        name="project",
    )(*chunks, out_weight)
    grads = [lax.ppermute(one, "seq", out_pairs(phase)) for phase, one in enumerate(grads)]

    lse, mean = pl.pallas_call(
        stats_kernel,
        in_specs=[SMEM] + [VMEM] * 9,
        out_specs=[VMEM] * 2,
        out_shape=[sds((1, QALL), F32), sds((DH, QALL), F32)],
        scratch_shapes=[
            pltpu.VMEM((12, TOK, DH), BF16),
            pltpu.VMEM((12, TOK, DH), BF16),
            pltpu.VMEM((QALL, DH), BF16),
            pltpu.VMEM((12, TOK, SPAN), F32),
            pltpu.VMEM((TEXT, QALL), F32),
            pltpu.VMEM((8, QALL), F32),
        ],
        compiler_params=params(24),
        cost_estimate=pl.CostEstimate(flops=1000, bytes_accessed=1000, transcendentals=0),
        name="softmax_stats",
    )(extents, *msgs, core_kv, time_kv, text_keys, text_values, text_bias)

    half_sum = sds((4, 2, TOK, DH), BF16)
    scratch = [
        pltpu.VMEM((4, TOK, DH), BF16),
        pltpu.VMEM((4, TOK, DH), BF16),
        pltpu.VMEM((QALL, DH), BF16),
    ]
    cost = pl.CostEstimate(flops=1000, bytes_accessed=1000, transcendentals=0)
    time_part, text_part, dq, delta, grad_rows = pl.pallas_call(
        time_grads_kernel,
        in_specs=[SMEM] + [VMEM] * 14,
        out_specs=[VMEM] * 5,
        out_shape=[
            half_sum,
            sds((TEXT, 2 * DH), BF16),
            sds((DH, QALL), F32),
            sds((1, QALL), F32),
            sds((QALL, DH), BF16),
        ],
        scratch_shapes=scratch,
        compiler_params=params(),
        cost_estimate=cost,
        name="far_grads",
    )(extents, *msgs, *grads, time_kv, lse, mean, text_keys, text_values, text_bias)
    time_back = lax.ppermute(time_part, "seq", time_pairs())
    core_part, own_part = pl.pallas_call(
        near_grads_kernel,
        in_specs=[SMEM] + [VMEM] * 9,
        out_specs=[VMEM] * 2,
        out_shape=[half_sum, sds((4, 3, TOK, DH), F32)],
        scratch_shapes=scratch + [pltpu.VMEM((DH, QALL), F32)],
        compiler_params=params(16),
        cost_estimate=cost,
        name="own_grads",
    )(extents, *msgs, core_kv, lse, dq, delta, grad_rows)
    text_part, own_part = lax.optimization_barrier((text_part, own_part))
    core_back = lax.ppermute(core_part, "seq", core_pairs())
    groups = [[y * 8 + z_hi * 2 + c for y in range(4) for c in range(2)] for z_hi in range(4)]
    text_back = lax.all_to_all(
        text_part.reshape(8, TEXT // 8, 2 * DH), "seq", 0, 0, axis_index_groups=groups
    )

    results = pl.pallas_call(
        combine_kernel,
        in_specs=[VMEM] * 4,
        out_specs=[VMEM] * 4,
        out_shape=[sds((MSG, DH), BF16)] * 4,
        scratch_shapes=[pltpu.VMEM((TEXT // 8, 2 * DH), F32)],
        compiler_params=params(),
        name="combine",
    )(own_part, core_back, time_back, text_back)
    results = [lax.ppermute(one, "seq", back_pairs(phase)) for phase, one in enumerate(results)]

    width = 3 * DH
    return pl.pallas_call(
        unpack_kernel,
        in_specs=[VMEM] * 4,
        out_specs=[VMEM] * 5,
        out_shape=[
            sds((TOK, width), BF16),
            sds((TOK, width), F32),
            sds((TOK, width), F32),
            sds((8, width), F32),
            sds((8, width), F32),
        ],
        scratch_shapes=[pltpu.VMEM((4, MSG, DH), BF16)],
        compiler_params=params(),
        name="unpack",
    )(*results)


def solution(mesh):
    return jax.shard_map(
        per_device,
        mesh=mesh,
        in_specs=(
            P("seq", "head"),
            P("seq", "head"),
            P("seq", "head"),
            P("seq", "head"),
            P("head", None),
            P(None, "head"),
            P(None, "head"),
            P("head", None),
            P(),
        ),
        out_specs=(P("seq", "head"),) * 5,
        check_vma=False,
    )
```

```python
import functools
import math

import jax
import jax.numpy as jnp
from jax import lax
from jax.experimental import pallas as pl
from jax.experimental.pallas import tpu as pltpu
from jax.sharding import PartitionSpec as P

DH = 128
TOK = 256
TEXT = 256
ROWS = 4
SPAN = 3 * TOK
QALL = ROWS * TOK
MSG = 3 * TOK + 16
INV_ROOT = DH ** (-0.5)
LOG2E = math.log2(math.e)
F32 = jnp.float32
BF16 = jnp.bfloat16
ANY = pl.BlockSpec(memory_space=pltpu.HBM)
VMEM = pl.BlockSpec(memory_space=pltpu.VMEM)
SMEM = pl.BlockSpec(memory_space=pltpu.SMEM)


def params(mib=12):
    return pltpu.CompilerParams(vmem_limit_bytes=mib * 1024 * 1024)


def sds(shape, dtype):
    return jax.ShapeDtypeStruct(shape, dtype)


def dot_nt(a, b):
    return lax.dot_general(a, b, (((1,), (1,)), ((), ())), preferred_element_type=F32)


def dot_nn(a, b):
    return lax.dot_general(a, b, (((1,), (0,)), ((), ())), preferred_element_type=F32)


def dot_tn(a, b):
    return lax.dot_general(a, b, (((0,), (0,)), ((), ())), preferred_element_type=F32)


def sent_head(phase, h):
    far, swap = (1, 0, 1, 0)[phase], phase // 2
    return ((h >> 1) ^ far) + 2 * ((h & 1) ^ swap)


def received_height(phase, chip):
    far, swap = (1, 0, 1, 0)[phase], phase // 2
    return 2 * ((chip & 1) ^ far) + ((chip >> 1) ^ swap)


def out_pairs(phase):
    pairs = []
    for y in range(4):
        for zt in range(2):
            for h in range(4):
                head = sent_head(phase, h)
                if head < 3:
                    pairs.append((y * 8 + zt * 4 + h, y * 8 + head * 2 + zt))
    return pairs


def pair_head(far, h):
    return ((h >> 1) ^ far) + 2 * (h & 1)


def pair_pairs(far):
    pairs = []
    for y in range(4):
        for zt in range(2):
            for h in range(4):
                head = pair_head(far, h)
                if head < 3:
                    pairs.append((y * 8 + zt * 4 + h, y * 8 + head * 2 + zt))
    return pairs


def back_pairs(phase):
    return [(b, a) for a, b in out_pairs(phase)]


def core_pairs():
    return [(s, s ^ 1) for s in range(32) if (s // 2) % 4 < 3]


def time_pairs():
    pairs = []
    for s in range(32):
        y, z_hi, c = s // 8, (s // 2) % 4, s % 2
        if z_hi < 3:
            other = y + 1 if c else y - 1
            if 0 <= other < 4:
                pairs.append((s, other * 8 + z_hi * 2 + 1 - c))
    return pairs


def head_pairs(dx, dz):
    return [(g, ((g // 4 + dz) % 2) * 4 + (g % 4 + dx) % 4) for g in range(8)]


def start_all(copies):
    for one in copies:
        one.start()


def wait_all(copies):
    for one in copies:
        one.wait()


def home_height():
    return lax.axis_index("seq") & 3


def work_chip():
    return (lax.axis_index("seq") >> 1) & 3


def pack_kernel(q_ref, k_ref, v_ref, q_next, k_next, v_next, far_out, near_out):
    h = home_height()
    core = h & 1
    mine = pl.ds(pl.multiple_of(core * TOK, TOK), TOK)
    theirs = pl.ds(pl.multiple_of((1 - core) * TOK, TOK), TOK)
    for far, out in ((1, far_out), (0, near_out)):
        head = jnp.minimum(pair_head(far, h), 2)
        columns = pl.ds(pl.multiple_of(head * DH, DH), DH)
        for which, (own, other) in enumerate(((q_ref, q_next), (k_ref, k_next), (v_ref, v_next))):
            out[which, mine, :] = own[:, columns]
            out[which, theirs, :] = other[:, columns]


def project_kernel(c0, c1, c2, c3, c4, c5, c6, c7, w_ref, keep, give):
    chunks = (c0, c1, c2, c3, c4, c5, c6, c7)
    g = lax.axis_index("head")
    h = home_height()
    gz, gx = lax.div(g, 4), lax.rem(g, 4)
    width = c0.shape[1]
    for which_out in range(4):
        far, other = which_out & 1, which_out >> 1
        head = jnp.minimum(pair_head(far, h ^ other), 2)
        rows = pl.ds(pl.multiple_of(head * DH, DH), DH)
        total = None
        for which, chunk in enumerate(chunks):
            dz, dx = which // 4, which % 4
            src = lax.rem(gz + dz, 2) * 4 + lax.rem(gx - dx + 4, 4)
            columns = pl.ds(pl.multiple_of(src * width, width), width)
            term = dot_nt(chunk[...], w_ref[rows, columns])
            total = term if total is None else total + term
        (give if other else keep)[far] = total.astype(BF16)


def assemble_kernel(keep, got, near, far):
    core = home_height() & 1
    mine = pl.ds(pl.multiple_of(core * TOK, TOK), TOK)
    theirs = pl.ds(pl.multiple_of((1 - core) * TOK, TOK), TOK)
    for which, out in enumerate((near, far)):
        out[mine, :] = keep[which]
        out[theirs, :] = got[which]


def pair_rows(chip):
    firsts = [2 * ((chip & 1) ^ far) for far in (1, 0)]
    return [(which, first, row, slice(row * TOK, (row + 1) * TOK)) for which, first in enumerate(firsts) for row in (0, 1)]


def window(ext_ref, chip):
    head = jnp.minimum(chip, 2)
    reach_t, reach_h, reach_w = ext_ref[head, 0], ext_ref[head, 1], ext_ref[head, 2]
    s = lax.axis_index("seq")
    y, c = lax.div(s, 8), lax.rem(s, 2)
    near = reach_t >= 1
    outside = ((y == 0) & (c == 0)) | ((y == 3) & (c == 1))
    return (True, near, near & jnp.logical_not(outside)), reach_h, reach_w >= 1


def span_bias(block_ok, reach_h, wide, key_h, first_h):
    lane = lax.broadcasted_iota(jnp.int32, (1, TOK), 1)
    left = lane < TOK // 2
    top, low = [], []
    for j in range(3):
        ok = jnp.abs(first_h + j - key_h) <= reach_h
        if block_ok is not True:
            ok = ok & block_ok
        same = jnp.where(ok, 0.0, -jnp.inf).astype(F32)
        cross = jnp.where(ok & wide, 0.0, -jnp.inf).astype(F32)
        top.append(jnp.where(left, same, cross))
        low.append(jnp.where(left, cross, same))
    return jnp.concatenate(top, 1), jnp.concatenate(low, 1)


def first_height(key_h):
    return jnp.clip(key_h - 1, 0, 1)


def fold(x, how):
    return how(x.reshape(x.shape[0] // 8, 8, x.shape[1]), 0)


def stats_kernel(
    ext_ref, m_far, m_near, core_kv, time_kv, tk_ref, tv_ref, tb_ref,
    lse_ref, mean_ref,
    kb, vb, qb, sb, st, run,
):
    chip = work_chip()
    msgs = (m_far, m_near)
    for which, first, row, part in pair_rows(chip):
        h = first + row
        qb[pl.ds(pl.multiple_of(h * TOK, TOK), TOK), :] = msgs[which][0, part]
        kb[h], vb[h] = msgs[which][1, part], msgs[which][2, part]
        kb[4 + h], vb[4 + h] = core_kv[which, 0, part], core_kv[which, 1, part]
        kb[8 + h], vb[8 + h] = time_kv[which, 0, part], time_kv[which, 1, part]
    block_ok, reach_h, wide = window(ext_ref, chip)
    head = jnp.minimum(chip, 2)
    columns = pl.ds(pl.multiple_of(head * DH, DH), DH)
    factor = INV_ROOT * LOG2E

    text = dot_nt(tk_ref[:, columns], qb[...]) * factor + tb_ref[...]
    st[...] = text
    run[...] = fold(text, jnp.max)

    for part in range(3):

        def first(key_h, carry, part=part):
            h0 = first_height(key_h)
            rows = pl.ds(pl.multiple_of(h0 * TOK, TOK), SPAN)
            top, low = span_bias(block_ok[part], reach_h, wide, key_h, h0)
            s = dot_nt(kb[part * 4 + key_h], qb[rows, :]) * factor
            a, b = s[: TOK // 2] + top, s[TOK // 2 :] + low
            sb[part * 4 + key_h, : TOK // 2] = a
            sb[part * 4 + key_h, TOK // 2 :] = b
            run[:, rows] = jnp.maximum(run[:, rows], jnp.maximum(fold(a, jnp.max), fold(b, jnp.max)))
            return carry

        lax.fori_loop(0, 4, first, 0, unroll=True)

    top_score = jnp.max(run[...], 0, keepdims=True)
    lse_ref[...] = top_score
    weights = jnp.exp2(st[...] - top_score)
    run[...] = fold(weights, jnp.sum)
    mean_ref[...] = dot_tn(tv_ref[:, columns], weights.astype(BF16))

    def second(block, carry):
        key_h = lax.rem(block, 4)
        rows = pl.ds(pl.multiple_of(first_height(key_h) * TOK, TOK), SPAN)
        weights = jnp.exp2(sb[block] - lse_ref[:, rows])
        run[:, rows] += fold(weights, jnp.sum)
        mean_ref[:, rows] += dot_tn(vb[block], weights.astype(BF16))
        return carry

    lax.fori_loop(0, 12, second, 0, unroll=4)
    total = jnp.sum(run[...], 0, keepdims=True)
    lse_ref[...] = top_score + jnp.log2(total)
    mean_ref[...] = mean_ref[...] / total


def block_terms(keys, values, query, grad, bias, delta, factor):
    s = dot_nt(keys, query) * factor
    if isinstance(bias, tuple):
        top, low = bias
        half = TOK // 2
        probs = jnp.concatenate([jnp.exp2(s[:half] + top), jnp.exp2(s[half:] + low)], 0)
    else:
        probs = jnp.exp2(s + bias)
    dprobs = dot_nt(values, grad)
    dscores = (probs * (dprobs - delta)).astype(BF16)
    return probs.astype(BF16), dscores


def place_rows(chip, far_rows, near_rows, out):
    for far, rows in ((1, far_rows), (0, near_rows)):
        first = 2 * ((chip & 1) ^ far)
        out[pl.ds(pl.multiple_of(first * TOK, 2 * TOK), 2 * TOK), :] = rows


def part_grads(part, m_refs, kv_ref, ext_ref, lse_ref, delta_ref, out_ref, dq_ref, kb, vb, qb, gb):
    chip = work_chip()
    for which, first, row, rows in pair_rows(chip):
        kb[first + row] = m_refs[which][1, rows] if part == 0 else kv_ref[which, 0, rows]
        vb[first + row] = m_refs[which][2, rows] if part == 0 else kv_ref[which, 1, rows]
    block_ok, reach_h, wide = window(ext_ref, chip)
    factor = INV_ROOT * LOG2E

    def body(key_h, carry):
        h0 = first_height(key_h)
        rows = pl.ds(pl.multiple_of(h0 * TOK, TOK), SPAN)
        top, low = span_bias(block_ok[part], reach_h, wide, key_h, h0)
        lse = lse_ref[:, rows]
        query, grad, keys = qb[rows, :], gb[rows, :], kb[key_h]
        probs, dscores = block_terms(
            keys, vb[key_h], query, grad, (top - lse, low - lse), delta_ref[:, rows], factor
        )
        out_ref[key_h, 0] = (dot_nn(dscores, query) * INV_ROOT).astype(out_ref.dtype)
        out_ref[key_h, 1] = dot_nn(probs, grad).astype(out_ref.dtype)
        dq_ref[:, rows] += dot_tn(keys, dscores)
        return carry

    lax.fori_loop(0, 4, body, 0, unroll=True)


def time_grads_kernel(
    ext_ref, m_far, m_near, g_far, g_near, time_kv, lse_ref, mean_ref, tk_ref, tv_ref, tb_ref,
    time_out, text_ref, dq_ref, delta_ref, gb,
    kb, vb, qb,
):
    chip = work_chip()
    m_refs = (m_far, m_near)
    place_rows(chip, m_far[0], m_near[0], qb)
    place_rows(chip, g_far[...], g_near[...], gb)
    delta_ref[...] = jnp.sum(gb[...].astype(F32).T * mean_ref[...], 0, keepdims=True)
    head = jnp.minimum(chip, 2)
    columns = pl.ds(pl.multiple_of(head * DH, DH), DH)
    keys = tk_ref[:, columns]
    probs, dscores = block_terms(
        keys, tv_ref[:, columns], qb[...], gb[...], tb_ref[...] - lse_ref[...], delta_ref[...],
        INV_ROOT * LOG2E,
    )
    dq_ref[...] = dot_tn(keys, dscores)
    text_ref[:, :DH] = (dot_nn(dscores, qb[...]) * INV_ROOT).astype(BF16)
    text_ref[:, DH:] = dot_nn(probs, gb[...]).astype(BF16)
    part_grads(2, m_refs, time_kv, ext_ref, lse_ref, delta_ref, time_out, dq_ref, kb, vb, qb, gb)


def near_grads_kernel(
    ext_ref, m_far, m_near, core_kv, lse_ref, dq_in, delta_ref, gb,
    core_out, own_out,
    kb, vb, qb, dq_run,
):
    m_refs = (m_far, m_near)
    place_rows(work_chip(), m_far[0], m_near[0], qb)
    dq_run[...] = dq_in[...]
    part_grads(1, m_refs, core_kv, ext_ref, lse_ref, delta_ref, core_out, dq_run, kb, vb, qb, gb)
    part_grads(0, m_refs, None, ext_ref, lse_ref, delta_ref, own_out, dq_run, kb, vb, qb, gb)
    for h in range(ROWS):
        own_out[h, 2] = dq_run[:, h * TOK : (h + 1) * TOK].T * INV_ROOT


def combine_kernel(own, core, time, text, o0, o1, o2, o3, text_sum):
    chip = work_chip()
    text_sum[...] = jnp.sum(text[...].astype(F32), 0)
    for phase, out in enumerate((o0, o1, o2, o3)):
        h = received_height(phase, chip)
        out[:TOK] = own[h, 2].astype(BF16)
        for which in range(2):
            total = own[h, which] + core[h, which].astype(F32) + time[h, which].astype(F32)
            out[(1 + which) * TOK : (2 + which) * TOK] = total.astype(BF16)
        share = text_sum[pl.ds(pl.multiple_of(h * 8, 8), 8), :]
        out[3 * TOK :] = jnp.concatenate([share[:, :DH], share[:, DH:]], 0).astype(BF16)


def unpack_kernel(r0, r1, r2, r3, dq, dk, dv, tk, tv, buf):
    h = home_height()
    for phase, src in enumerate((r0, r1, r2, r3)):
        buf[sent_head(phase, h)] = src[...]
    for head in range(3):
        columns = slice(head * DH, (head + 1) * DH)
        dq[:, columns] = buf[head, :TOK]
        dk[:, columns] = buf[head, TOK : 2 * TOK].astype(F32)
        dv[:, columns] = buf[head, 2 * TOK : 3 * TOK].astype(F32)
        share = buf[head, 3 * TOK :].astype(F32)
        tk[:, columns] = share[:8]
        tv[:, columns] = share[8:]


def per_device(queries, keys, values, layer_grad, out_weight, text_keys, text_values, extents, text_mask):
    text_bias = jnp.where(text_mask == 1, 0.0, -jnp.inf).astype(F32)[:, None]

    beside = lax.ppermute(layer_grad, "head", head_pairs(0, 1))
    chunks = [
        src if dx == 0 else lax.ppermute(src, "head", head_pairs(dx, 0))
        for src in (layer_grad, beside)
        for dx in range(4)
    ]
    both = [(s, s ^ 1) for s in range(32)]
    inputs = (queries, keys, values)
    packed = pl.pallas_call(
        pack_kernel,
        in_specs=[VMEM] * 6,
        out_specs=[VMEM] * 2,
        out_shape=[sds((3, 2 * TOK, DH), BF16)] * 2,
        compiler_params=params(),
        name="pack_heads",
    )(*inputs, *(lax.ppermute(one, "seq", both) for one in inputs))
    packed = list(packed)
    packed[1], chunks[1] = lax.optimization_barrier((packed[1], chunks[1]))
    msgs = [lax.ppermute(one, "seq", pair_pairs(which)) for which, one in zip((1, 0), packed)]
    msgs, chunks = lax.optimization_barrier((msgs, chunks))
    kv = jnp.stack([one[1:] for one in msgs])
    core_kv = lax.ppermute(kv, "seq", core_pairs())
    time_kv = lax.ppermute(kv, "seq", time_pairs())

    keep, give = pl.pallas_call(
        project_kernel,
        in_specs=[VMEM] * 9,
        out_specs=[VMEM] * 2,
        out_shape=[sds((2, TOK, DH), BF16)] * 2,
        compiler_params=params(),
        name="project",
    )(*chunks, out_weight)
    got = lax.ppermute(give, "seq", both)
    near, far = pl.pallas_call(
        assemble_kernel,
        in_specs=[VMEM] * 2,
        out_specs=[VMEM] * 2,
        out_shape=[sds((2 * TOK, DH), BF16)] * 2,
        compiler_params=params(),
        name="assemble",
    )(keep, got)
    grads = [lax.ppermute(one, "seq", pair_pairs(which)) for which, one in ((1, far), (0, near))]

    lse, mean = pl.pallas_call(
        stats_kernel,
        in_specs=[SMEM] + [VMEM] * 7,
        out_specs=[VMEM] * 2,
        out_shape=[sds((1, QALL), F32), sds((DH, QALL), F32)],
        scratch_shapes=[
            pltpu.VMEM((12, TOK, DH), BF16),
            pltpu.VMEM((12, TOK, DH), BF16),
            pltpu.VMEM((QALL, DH), BF16),
            pltpu.VMEM((12, TOK, SPAN), F32),
            pltpu.VMEM((TEXT, QALL), F32),
            pltpu.VMEM((8, QALL), F32),
        ],
        compiler_params=params(24),
        cost_estimate=pl.CostEstimate(flops=1000, bytes_accessed=1000, transcendentals=0),
        name="softmax_stats",
    )(extents, *msgs, core_kv, time_kv, text_keys, text_values, text_bias)

    half_sum = sds((4, 2, TOK, DH), BF16)
    scratch = [
        pltpu.VMEM((4, TOK, DH), BF16),
        pltpu.VMEM((4, TOK, DH), BF16),
        pltpu.VMEM((QALL, DH), BF16),
    ]
    cost = pl.CostEstimate(flops=1000, bytes_accessed=1000, transcendentals=0)
    time_part, text_part, dq, delta, grad_rows = pl.pallas_call(
        time_grads_kernel,
        in_specs=[SMEM] + [VMEM] * 10,
        out_specs=[VMEM] * 5,
        out_shape=[
            half_sum,
            sds((TEXT, 2 * DH), BF16),
            sds((DH, QALL), F32),
            sds((1, QALL), F32),
            sds((QALL, DH), BF16),
        ],
        scratch_shapes=scratch,
        compiler_params=params(),
        cost_estimate=cost,
        name="far_grads",
    )(extents, *msgs, *grads, time_kv, lse, mean, text_keys, text_values, text_bias)
    time_back = lax.ppermute(time_part, "seq", time_pairs())
    core_part, own_part = pl.pallas_call(
        near_grads_kernel,
        in_specs=[SMEM] + [VMEM] * 7,
        out_specs=[VMEM] * 2,
        out_shape=[half_sum, sds((4, 3, TOK, DH), F32)],
        scratch_shapes=scratch + [pltpu.VMEM((DH, QALL), F32)],
        compiler_params=params(16),
        cost_estimate=cost,
        name="own_grads",
    )(extents, *msgs, core_kv, lse, dq, delta, grad_rows)
    text_part, own_part = lax.optimization_barrier((text_part, own_part))
    core_back = lax.ppermute(core_part, "seq", core_pairs())
    groups = [[y * 8 + z_hi * 2 + c for y in range(4) for c in range(2)] for z_hi in range(4)]
    text_back = lax.all_to_all(
        text_part.reshape(8, TEXT // 8, 2 * DH), "seq", 0, 0, axis_index_groups=groups
    )

    results = pl.pallas_call(
        combine_kernel,
        in_specs=[VMEM] * 4,
        out_specs=[VMEM] * 4,
        out_shape=[sds((MSG, DH), BF16)] * 4,
        scratch_shapes=[pltpu.VMEM((TEXT // 8, 2 * DH), F32)],
        compiler_params=params(),
        name="combine",
    )(own_part, core_back, time_back, text_back)
    results = [lax.ppermute(one, "seq", back_pairs(phase)) for phase, one in enumerate(results)]

    width = 3 * DH
    return pl.pallas_call(
        unpack_kernel,
        in_specs=[VMEM] * 4,
        out_specs=[VMEM] * 5,
        out_shape=[
            sds((TOK, width), BF16),
            sds((TOK, width), F32),
            sds((TOK, width), F32),
            sds((8, width), F32),
            sds((8, width), F32),
        ],
        scratch_shapes=[pltpu.VMEM((4, MSG, DH), BF16)],
        compiler_params=params(),
        name="unpack",
    )(*results)


def solution(mesh):
    return jax.shard_map(
        per_device,
        mesh=mesh,
        in_specs=(
            P("seq", "head"),
            P("seq", "head"),
            P("seq", "head"),
            P("seq", "head"),
            P("head", None),
            P(None, "head"),
            P(None, "head"),
            P("head", None),
            P(),
        ),
        out_specs=(P("seq", "head"),) * 5,
        check_vma=False,
    )
```

```python
import functools
import math

import jax
import jax.numpy as jnp
from jax import lax
from jax.experimental import pallas as pl
from jax.experimental.pallas import tpu as pltpu
from jax.sharding import PartitionSpec as P

DH = 128
TOK = 256
TEXT = 256
ROWS = 4
SPAN = 3 * TOK
QALL = ROWS * TOK
MSG = 3 * TOK + 16
INV_ROOT = DH ** (-0.5)
LOG2E = math.log2(math.e)
F32 = jnp.float32
BF16 = jnp.bfloat16
ANY = pl.BlockSpec(memory_space=pltpu.HBM)
VMEM = pl.BlockSpec(memory_space=pltpu.VMEM)
SMEM = pl.BlockSpec(memory_space=pltpu.SMEM)


def params(mib=12):
    return pltpu.CompilerParams(vmem_limit_bytes=mib * 1024 * 1024)


def sds(shape, dtype):
    return jax.ShapeDtypeStruct(shape, dtype)


def dot_nt(a, b):
    return lax.dot_general(a, b, (((1,), (1,)), ((), ())), preferred_element_type=F32)


def dot_nn(a, b):
    return lax.dot_general(a, b, (((1,), (0,)), ((), ())), preferred_element_type=F32)


def dot_tn(a, b):
    return lax.dot_general(a, b, (((0,), (0,)), ((), ())), preferred_element_type=F32)


def sent_head(phase, h):
    far, swap = (1, 0, 1, 0)[phase], phase // 2
    return ((h >> 1) ^ far) + 2 * ((h & 1) ^ swap)


def received_height(phase, chip):
    far, swap = (1, 0, 1, 0)[phase], phase // 2
    return 2 * ((chip & 1) ^ far) + ((chip >> 1) ^ swap)


def out_pairs(phase):
    pairs = []
    for y in range(4):
        for zt in range(2):
            for h in range(4):
                head = sent_head(phase, h)
                if head < 3:
                    pairs.append((y * 8 + zt * 4 + h, y * 8 + head * 2 + zt))
    return pairs


def pair_head(far, h):
    return ((h >> 1) ^ far) + 2 * (h & 1)


def pair_pairs(far):
    pairs = []
    for y in range(4):
        for zt in range(2):
            for h in range(4):
                head = pair_head(far, h)
                if head < 3:
                    pairs.append((y * 8 + zt * 4 + h, y * 8 + head * 2 + zt))
    return pairs


def back_pairs(phase):
    return [(b, a) for a, b in out_pairs(phase)]


def core_pairs():
    return [(s, s ^ 1) for s in range(32) if (s // 2) % 4 < 3]


def time_pairs():
    pairs = []
    for s in range(32):
        y, z_hi, c = s // 8, (s // 2) % 4, s % 2
        if z_hi < 3:
            other = y + 1 if c else y - 1
            if 0 <= other < 4:
                pairs.append((s, other * 8 + z_hi * 2 + 1 - c))
    return pairs


def head_pairs(dx, dz):
    return [(g, ((g // 4 + dz) % 2) * 4 + (g % 4 + dx) % 4) for g in range(8)]


def start_all(copies):
    for one in copies:
        one.start()


def wait_all(copies):
    for one in copies:
        one.wait()


def home_height():
    return lax.axis_index("seq") & 3


def work_chip():
    return (lax.axis_index("seq") >> 1) & 3


def pack_kernel(q_ref, k_ref, v_ref, q_next, k_next, v_next, far_out, near_out):
    h = home_height()
    core = h & 1
    mine = pl.ds(pl.multiple_of(core * TOK, TOK), TOK)
    theirs = pl.ds(pl.multiple_of((1 - core) * TOK, TOK), TOK)
    for far, out in ((1, far_out), (0, near_out)):
        head = jnp.minimum(pair_head(far, h), 2)
        columns = pl.ds(pl.multiple_of(head * DH, DH), DH)
        for which, (own, other) in enumerate(((q_ref, q_next), (k_ref, k_next), (v_ref, v_next))):
            out[which, mine, :] = own[:, columns]
            out[which, theirs, :] = other[:, columns]


def project_terms(chunks, dz, w_ref, which_out):
    g = lax.axis_index("head")
    gz, gx = lax.div(g, 4), lax.rem(g, 4)
    h = home_height()
    width = chunks[0].shape[1]
    far, other = which_out & 1, which_out >> 1
    head = jnp.minimum(pair_head(far, h ^ other), 2)
    rows = pl.ds(pl.multiple_of(head * DH, DH), DH)
    total = None
    for dx, chunk in enumerate(chunks):
        src = lax.rem(gz + dz, 2) * 4 + lax.rem(gx - dx + 4, 4)
        columns = pl.ds(pl.multiple_of(src * width, width), width)
        term = dot_nt(chunk[...], w_ref[rows, columns])
        total = term if total is None else total + term
    return total


def project_first_kernel(c0, c1, c2, c3, w_ref, acc):
    for which_out in range(4):
        acc[which_out] = project_terms((c0, c1, c2, c3), 0, w_ref, which_out)


def project_kernel(c4, c5, c6, c7, w_ref, acc, keep, give):
    for which_out in range(4):
        total = acc[which_out] + project_terms((c4, c5, c6, c7), 1, w_ref, which_out)
        (give if which_out >> 1 else keep)[which_out & 1] = total.astype(BF16)


def assemble_kernel(keep, got, near, far):
    core = home_height() & 1
    mine = pl.ds(pl.multiple_of(core * TOK, TOK), TOK)
    theirs = pl.ds(pl.multiple_of((1 - core) * TOK, TOK), TOK)
    for which, out in enumerate((near, far)):
        out[mine, :] = keep[which]
        out[theirs, :] = got[which]


def pair_rows(chip):
    firsts = [2 * ((chip & 1) ^ far) for far in (1, 0)]
    return [(which, first, row, slice(row * TOK, (row + 1) * TOK)) for which, first in enumerate(firsts) for row in (0, 1)]


def window(ext_ref, chip):
    head = jnp.minimum(chip, 2)
    reach_t, reach_h, reach_w = ext_ref[head, 0], ext_ref[head, 1], ext_ref[head, 2]
    s = lax.axis_index("seq")
    y, c = lax.div(s, 8), lax.rem(s, 2)
    near = reach_t >= 1
    outside = ((y == 0) & (c == 0)) | ((y == 3) & (c == 1))
    return (True, near, near & jnp.logical_not(outside)), reach_h, reach_w >= 1


def span_bias(block_ok, reach_h, wide, key_h, first_h):
    lane = lax.broadcasted_iota(jnp.int32, (1, TOK), 1)
    left = lane < TOK // 2
    top, low = [], []
    for j in range(3):
        ok = jnp.abs(first_h + j - key_h) <= reach_h
        if block_ok is not True:
            ok = ok & block_ok
        same = jnp.where(ok, 0.0, -jnp.inf).astype(F32)
        cross = jnp.where(ok & wide, 0.0, -jnp.inf).astype(F32)
        top.append(jnp.where(left, same, cross))
        low.append(jnp.where(left, cross, same))
    return jnp.concatenate(top, 1), jnp.concatenate(low, 1)


def first_height(key_h):
    return jnp.clip(key_h - 1, 0, 1)


def fold(x, how):
    return how(x.reshape(x.shape[0] // 8, 8, x.shape[1]), 0)


def stats_kernel(
    ext_ref, m_far, m_near, core_kv, time_kv, tk_ref, tv_ref, tb_ref,
    lse_ref, mean_ref,
    kb, vb, qb, sb, st, run,
):
    chip = work_chip()
    msgs = (m_far, m_near)
    for which, first, row, part in pair_rows(chip):
        h = first + row
        qb[pl.ds(pl.multiple_of(h * TOK, TOK), TOK), :] = msgs[which][0, part]
        kb[h], vb[h] = msgs[which][1, part], msgs[which][2, part]
        kb[4 + h], vb[4 + h] = core_kv[which, 0, part], core_kv[which, 1, part]
        kb[8 + h], vb[8 + h] = time_kv[which, 0, part], time_kv[which, 1, part]
    block_ok, reach_h, wide = window(ext_ref, chip)
    head = jnp.minimum(chip, 2)
    columns = pl.ds(pl.multiple_of(head * DH, DH), DH)
    factor = INV_ROOT * LOG2E

    text = dot_nt(tk_ref[:, columns], qb[...]) * factor + tb_ref[...]
    st[...] = text
    run[...] = fold(text, jnp.max)

    for part in range(3):

        def first(key_h, carry, part=part):
            h0 = first_height(key_h)
            rows = pl.ds(pl.multiple_of(h0 * TOK, TOK), SPAN)
            top, low = span_bias(block_ok[part], reach_h, wide, key_h, h0)
            s = dot_nt(kb[part * 4 + key_h], qb[rows, :]) * factor
            a, b = s[: TOK // 2] + top, s[TOK // 2 :] + low
            sb[part * 4 + key_h, : TOK // 2] = a
            sb[part * 4 + key_h, TOK // 2 :] = b
            run[:, rows] = jnp.maximum(run[:, rows], jnp.maximum(fold(a, jnp.max), fold(b, jnp.max)))
            return carry

        lax.fori_loop(0, 4, first, 0, unroll=True)

    top_score = jnp.max(run[...], 0, keepdims=True)
    lse_ref[...] = top_score
    weights = jnp.exp2(st[...] - top_score)
    run[...] = fold(weights, jnp.sum)
    mean_ref[...] = dot_tn(tv_ref[:, columns], weights.astype(BF16))

    def second(block, carry):
        key_h = lax.rem(block, 4)
        rows = pl.ds(pl.multiple_of(first_height(key_h) * TOK, TOK), SPAN)
        weights = jnp.exp2(sb[block] - lse_ref[:, rows])
        run[:, rows] += fold(weights, jnp.sum)
        mean_ref[:, rows] += dot_tn(vb[block], weights.astype(BF16))
        return carry

    lax.fori_loop(0, 12, second, 0, unroll=4)
    total = jnp.sum(run[...], 0, keepdims=True)
    lse_ref[...] = top_score + jnp.log2(total)
    mean_ref[...] = mean_ref[...] / total


def block_terms(keys, values, query, grad, bias, delta, factor):
    s = dot_nt(keys, query) * factor
    if isinstance(bias, tuple):
        top, low = bias
        half = TOK // 2
        probs = jnp.concatenate([jnp.exp2(s[:half] + top), jnp.exp2(s[half:] + low)], 0)
    else:
        probs = jnp.exp2(s + bias)
    dprobs = dot_nt(values, grad)
    dscores = (probs * (dprobs - delta)).astype(BF16)
    return probs.astype(BF16), dscores


def place_rows(chip, far_rows, near_rows, out):
    for far, rows in ((1, far_rows), (0, near_rows)):
        first = 2 * ((chip & 1) ^ far)
        out[pl.ds(pl.multiple_of(first * TOK, 2 * TOK), 2 * TOK), :] = rows


def part_grads(part, m_refs, kv_ref, ext_ref, lse_ref, delta_ref, out_ref, dq_ref, kb, vb, qb, gb):
    chip = work_chip()
    for which, first, row, rows in pair_rows(chip):
        kb[first + row] = m_refs[which][1, rows] if part == 0 else kv_ref[which, 0, rows]
        vb[first + row] = m_refs[which][2, rows] if part == 0 else kv_ref[which, 1, rows]
    block_ok, reach_h, wide = window(ext_ref, chip)
    factor = INV_ROOT * LOG2E

    def body(key_h, carry):
        h0 = first_height(key_h)
        rows = pl.ds(pl.multiple_of(h0 * TOK, TOK), SPAN)
        top, low = span_bias(block_ok[part], reach_h, wide, key_h, h0)
        lse = lse_ref[:, rows]
        query, grad, keys = qb[rows, :], gb[rows, :], kb[key_h]
        probs, dscores = block_terms(
            keys, vb[key_h], query, grad, (top - lse, low - lse), delta_ref[:, rows], factor
        )
        out_ref[key_h, 0] = (dot_nn(dscores, query) * INV_ROOT).astype(out_ref.dtype)
        out_ref[key_h, 1] = dot_nn(probs, grad).astype(out_ref.dtype)
        dq_ref[:, rows] += dot_tn(keys, dscores)
        return carry

    lax.fori_loop(0, 4, body, 0, unroll=True)


def time_grads_kernel(
    ext_ref, m_far, m_near, g_far, g_near, time_kv, lse_ref, mean_ref, tk_ref, tv_ref, tb_ref,
    time_out, text_ref, dq_ref, delta_ref, gb,
    kb, vb, qb,
):
    chip = work_chip()
    m_refs = (m_far, m_near)
    place_rows(chip, m_far[0], m_near[0], qb)
    place_rows(chip, g_far[...], g_near[...], gb)
    delta_ref[...] = jnp.sum(gb[...].astype(F32).T * mean_ref[...], 0, keepdims=True)
    head = jnp.minimum(chip, 2)
    columns = pl.ds(pl.multiple_of(head * DH, DH), DH)
    keys = tk_ref[:, columns]
    probs, dscores = block_terms(
        keys, tv_ref[:, columns], qb[...], gb[...], tb_ref[...] - lse_ref[...], delta_ref[...],
        INV_ROOT * LOG2E,
    )
    dq_ref[...] = dot_tn(keys, dscores)
    text_ref[:, :DH] = (dot_nn(dscores, qb[...]) * INV_ROOT).astype(BF16)
    text_ref[:, DH:] = dot_nn(probs, gb[...]).astype(BF16)
    part_grads(2, m_refs, time_kv, ext_ref, lse_ref, delta_ref, time_out, dq_ref, kb, vb, qb, gb)


def near_grads_kernel(
    ext_ref, m_far, m_near, core_kv, lse_ref, dq_in, delta_ref, gb,
    core_out, own_out,
    kb, vb, qb, dq_run,
):
    m_refs = (m_far, m_near)
    place_rows(work_chip(), m_far[0], m_near[0], qb)
    dq_run[...] = dq_in[...]
    part_grads(1, m_refs, core_kv, ext_ref, lse_ref, delta_ref, core_out, dq_run, kb, vb, qb, gb)
    part_grads(0, m_refs, None, ext_ref, lse_ref, delta_ref, own_out, dq_run, kb, vb, qb, gb)
    for h in range(ROWS):
        own_out[h, 2] = dq_run[:, h * TOK : (h + 1) * TOK].T * INV_ROOT


def combine_kernel(own, core, time, text, o0, o1, o2, o3, text_sum):
    chip = work_chip()
    text_sum[...] = jnp.sum(text[...].astype(F32), 0)
    for phase, out in enumerate((o0, o1, o2, o3)):
        h = received_height(phase, chip)
        out[:TOK] = own[h, 2].astype(BF16)
        for which in range(2):
            total = own[h, which] + core[h, which].astype(F32) + time[h, which].astype(F32)
            out[(1 + which) * TOK : (2 + which) * TOK] = total.astype(BF16)
        share = text_sum[pl.ds(pl.multiple_of(h * 8, 8), 8), :]
        out[3 * TOK :] = jnp.concatenate([share[:, :DH], share[:, DH:]], 0).astype(BF16)


def unpack_kernel(r0, r1, r2, r3, dq, dk, dv, tk, tv, buf):
    h = home_height()
    for phase, src in enumerate((r0, r1, r2, r3)):
        buf[sent_head(phase, h)] = src[...]
    for head in range(3):
        columns = slice(head * DH, (head + 1) * DH)
        dq[:, columns] = buf[head, :TOK]
        dk[:, columns] = buf[head, TOK : 2 * TOK].astype(F32)
        dv[:, columns] = buf[head, 2 * TOK : 3 * TOK].astype(F32)
        share = buf[head, 3 * TOK :].astype(F32)
        tk[:, columns] = share[:8]
        tv[:, columns] = share[8:]


def per_device(queries, keys, values, layer_grad, out_weight, text_keys, text_values, extents, text_mask):
    text_bias = jnp.where(text_mask == 1, 0.0, -jnp.inf).astype(F32)[:, None]

    beside = lax.ppermute(layer_grad, "head", head_pairs(0, 1))
    chunks = [
        src if dx == 0 else lax.ppermute(src, "head", head_pairs(dx, 0))
        for src in (layer_grad, beside)
        for dx in range(4)
    ]
    both = [(s, s ^ 1) for s in range(32)]
    inputs = (queries, keys, values)
    packed = pl.pallas_call(
        pack_kernel,
        in_specs=[VMEM] * 6,
        out_specs=[VMEM] * 2,
        out_shape=[sds((3, 2 * TOK, DH), BF16)] * 2,
        compiler_params=params(),
        name="pack_heads",
    )(*inputs, *(lax.ppermute(one, "seq", both) for one in inputs))
    packed = list(packed)
    msgs = [lax.ppermute(one, "seq", pair_pairs(which)) for which, one in zip((1, 0), packed)]
    partial = pl.pallas_call(
        project_first_kernel,
        in_specs=[VMEM] * 5,
        out_specs=VMEM,
        out_shape=sds((4, TOK, DH), F32),
        compiler_params=params(),
        name="project_first",
    )(*chunks[:4], out_weight)
    keep, give = pl.pallas_call(
        project_kernel,
        in_specs=[VMEM] * 6,
        out_specs=[VMEM] * 2,
        out_shape=[sds((2, TOK, DH), BF16)] * 2,
        compiler_params=params(),
        name="project",
    )(*chunks[4:], out_weight, partial)
    got = lax.ppermute(give, "seq", both)
    msgs, got = lax.optimization_barrier((msgs, got))
    kv = jnp.stack([one[1:] for one in msgs])
    core_kv = lax.ppermute(kv, "seq", core_pairs())
    time_kv = lax.ppermute(kv, "seq", time_pairs())

    near, far = pl.pallas_call(
        assemble_kernel,
        in_specs=[VMEM] * 2,
        out_specs=[VMEM] * 2,
        out_shape=[sds((2 * TOK, DH), BF16)] * 2,
        compiler_params=params(),
        name="assemble",
    )(keep, got)
    grads = [lax.ppermute(one, "seq", pair_pairs(which)) for which, one in ((1, far), (0, near))]

    lse, mean = pl.pallas_call(
        stats_kernel,
        in_specs=[SMEM] + [VMEM] * 7,
        out_specs=[VMEM] * 2,
        out_shape=[sds((1, QALL), F32), sds((DH, QALL), F32)],
        scratch_shapes=[
            pltpu.VMEM((12, TOK, DH), BF16),
            pltpu.VMEM((12, TOK, DH), BF16),
            pltpu.VMEM((QALL, DH), BF16),
            pltpu.VMEM((12, TOK, SPAN), F32),
            pltpu.VMEM((TEXT, QALL), F32),
            pltpu.VMEM((8, QALL), F32),
        ],
        compiler_params=params(24),
        cost_estimate=pl.CostEstimate(flops=1000, bytes_accessed=1000, transcendentals=0),
        name="softmax_stats",
    )(extents, *msgs, core_kv, time_kv, text_keys, text_values, text_bias)

    half_sum = sds((4, 2, TOK, DH), BF16)
    scratch = [
        pltpu.VMEM((4, TOK, DH), BF16),
        pltpu.VMEM((4, TOK, DH), BF16),
        pltpu.VMEM((QALL, DH), BF16),
    ]
    cost = pl.CostEstimate(flops=1000, bytes_accessed=1000, transcendentals=0)
    time_part, text_part, dq, delta, grad_rows = pl.pallas_call(
        time_grads_kernel,
        in_specs=[SMEM] + [VMEM] * 10,
        out_specs=[VMEM] * 5,
        out_shape=[
            half_sum,
            sds((TEXT, 2 * DH), BF16),
            sds((DH, QALL), F32),
            sds((1, QALL), F32),
            sds((QALL, DH), BF16),
        ],
        scratch_shapes=scratch,
        compiler_params=params(),
        cost_estimate=cost,
        name="far_grads",
    )(extents, *msgs, *grads, time_kv, lse, mean, text_keys, text_values, text_bias)
    time_back = lax.ppermute(time_part, "seq", time_pairs())
    core_part, own_part = pl.pallas_call(
        near_grads_kernel,
        in_specs=[SMEM] + [VMEM] * 7,
        out_specs=[VMEM] * 2,
        out_shape=[half_sum, sds((4, 3, TOK, DH), F32)],
        scratch_shapes=scratch + [pltpu.VMEM((DH, QALL), F32)],
        compiler_params=params(16),
        cost_estimate=cost,
        name="own_grads",
    )(extents, *msgs, core_kv, lse, dq, delta, grad_rows)
    text_part, own_part = lax.optimization_barrier((text_part, own_part))
    core_back = lax.ppermute(core_part, "seq", core_pairs())
    groups = [[y * 8 + z_hi * 2 + c for y in range(4) for c in range(2)] for z_hi in range(4)]
    text_back = lax.all_to_all(
        text_part.reshape(8, TEXT // 8, 2 * DH), "seq", 0, 0, axis_index_groups=groups
    )

    results = pl.pallas_call(
        combine_kernel,
        in_specs=[VMEM] * 4,
        out_specs=[VMEM] * 4,
        out_shape=[sds((MSG, DH), BF16)] * 4,
        scratch_shapes=[pltpu.VMEM((TEXT // 8, 2 * DH), F32)],
        compiler_params=params(),
        name="combine",
    )(own_part, core_back, time_back, text_back)
    results = [lax.ppermute(one, "seq", back_pairs(phase)) for phase, one in enumerate(results)]

    width = 3 * DH
    return pl.pallas_call(
        unpack_kernel,
        in_specs=[VMEM] * 4,
        out_specs=[VMEM] * 5,
        out_shape=[
            sds((TOK, width), BF16),
            sds((TOK, width), F32),
            sds((TOK, width), F32),
            sds((8, width), F32),
            sds((8, width), F32),
        ],
        scratch_shapes=[pltpu.VMEM((4, MSG, DH), BF16)],
        compiler_params=params(),
        name="unpack",
    )(*results)


def solution(mesh):
    return jax.shard_map(
        per_device,
        mesh=mesh,
        in_specs=(
            P("seq", "head"),
            P("seq", "head"),
            P("seq", "head"),
            P("seq", "head"),
            P("head", None),
            P(None, "head"),
            P(None, "head"),
            P("head", None),
            P(),
        ),
        out_specs=(P("seq", "head"),) * 5,
        check_vma=False,
    )
```

```python
import functools
import math

import jax
import jax.numpy as jnp
from jax import lax
from jax.experimental import pallas as pl
from jax.experimental.pallas import tpu as pltpu
from jax.sharding import PartitionSpec as P

DH = 128
TOK = 256
TEXT = 256
ROWS = 4
SPAN = 3 * TOK
QALL = ROWS * TOK
MSG = 3 * TOK + 16
INV_ROOT = DH ** (-0.5)
LOG2E = math.log2(math.e)
F32 = jnp.float32
BF16 = jnp.bfloat16
ANY = pl.BlockSpec(memory_space=pltpu.HBM)
VMEM = pl.BlockSpec(memory_space=pltpu.VMEM)
SMEM = pl.BlockSpec(memory_space=pltpu.SMEM)


def params(mib=12):
    return pltpu.CompilerParams(vmem_limit_bytes=mib * 1024 * 1024)


def sds(shape, dtype):
    return jax.ShapeDtypeStruct(shape, dtype)


def dot_nt(a, b):
    return lax.dot_general(a, b, (((1,), (1,)), ((), ())), preferred_element_type=F32)


def dot_nn(a, b):
    return lax.dot_general(a, b, (((1,), (0,)), ((), ())), preferred_element_type=F32)


def dot_tn(a, b):
    return lax.dot_general(a, b, (((0,), (0,)), ((), ())), preferred_element_type=F32)


def sent_head(phase, h):
    far, swap = (1, 0, 1, 0)[phase], phase // 2
    return ((h >> 1) ^ far) + 2 * ((h & 1) ^ swap)


def received_height(phase, chip):
    far, swap = (1, 0, 1, 0)[phase], phase // 2
    return 2 * ((chip & 1) ^ far) + ((chip >> 1) ^ swap)


def out_pairs(phase):
    pairs = []
    for y in range(4):
        for zt in range(2):
            for h in range(4):
                head = sent_head(phase, h)
                if head < 3:
                    pairs.append((y * 8 + zt * 4 + h, y * 8 + head * 2 + zt))
    return pairs


def pair_head(far, h):
    return ((h >> 1) ^ far) + 2 * (h & 1)


def pair_pairs(far):
    pairs = []
    for y in range(4):
        for zt in range(2):
            for h in range(4):
                head = pair_head(far, h)
                if head < 3:
                    pairs.append((y * 8 + zt * 4 + h, y * 8 + head * 2 + zt))
    return pairs


def back_pairs(phase):
    return [(b, a) for a, b in out_pairs(phase)]


def core_pairs():
    return [(s, s ^ 1) for s in range(32) if (s // 2) % 4 < 3]


def time_pairs():
    pairs = []
    for s in range(32):
        y, z_hi, c = s // 8, (s // 2) % 4, s % 2
        if z_hi < 3:
            other = y + 1 if c else y - 1
            if 0 <= other < 4:
                pairs.append((s, other * 8 + z_hi * 2 + 1 - c))
    return pairs


def head_pairs(dx, dz):
    return [(g, ((g // 4 + dz) % 2) * 4 + (g % 4 + dx) % 4) for g in range(8)]


def start_all(copies):
    for one in copies:
        one.start()


def wait_all(copies):
    for one in copies:
        one.wait()


def home_height():
    return lax.axis_index("seq") & 3


def work_chip():
    return (lax.axis_index("seq") >> 1) & 3


def pack_kernel(q_ref, k_ref, v_ref, q_next, k_next, v_next, far_out, near_out, q_own, k_own, v_own, sem):
    pairs = ((q_ref, q_own), (k_ref, k_own), (v_ref, v_own))
    copies = [pltpu.make_async_copy(src, dst, sem.at[i]) for i, (src, dst) in enumerate(pairs)]
    start_all(copies)
    h = home_height()
    core = h & 1
    mine = pl.ds(pl.multiple_of(core * TOK, TOK), TOK)
    theirs = pl.ds(pl.multiple_of((1 - core) * TOK, TOK), TOK)
    wait_all(copies)
    for far, out in ((1, far_out), (0, near_out)):
        head = jnp.minimum(pair_head(far, h), 2)
        columns = pl.ds(pl.multiple_of(head * DH, DH), DH)
        for which, (own, other) in enumerate(((q_own, q_next), (k_own, k_next), (v_own, v_next))):
            out[which, mine, :] = own[:, columns]
            out[which, theirs, :] = other[:, columns]


def project_terms(chunks, dz, w_ref, which_out):
    g = lax.axis_index("head")
    gz, gx = lax.div(g, 4), lax.rem(g, 4)
    h = home_height()
    width = chunks[0].shape[1]
    far, other = which_out & 1, which_out >> 1
    head = jnp.minimum(pair_head(far, h ^ other), 2)
    rows = pl.ds(pl.multiple_of(head * DH, DH), DH)
    total = None
    for dx, chunk in enumerate(chunks):
        src = lax.rem(gz + dz, 2) * 4 + lax.rem(gx - dx + 4, 4)
        columns = pl.ds(pl.multiple_of(src * width, width), width)
        term = dot_nt(chunk[...], w_ref[rows, columns])
        total = term if total is None else total + term
    return total


def project_first_kernel(c0, c1, c2, c3, w_ref, acc):
    for which_out in range(4):
        acc[which_out] = project_terms((c0, c1, c2, c3), 0, w_ref, which_out)


def project_kernel(c4, c5, c6, c7, w_ref, acc, keep, give):
    for which_out in range(4):
        total = acc[which_out] + project_terms((c4, c5, c6, c7), 1, w_ref, which_out)
        (give if which_out >> 1 else keep)[which_out & 1] = total.astype(BF16)


def assemble_kernel(keep, got, near, far):
    core = home_height() & 1
    mine = pl.ds(pl.multiple_of(core * TOK, TOK), TOK)
    theirs = pl.ds(pl.multiple_of((1 - core) * TOK, TOK), TOK)
    for which, out in enumerate((near, far)):
        out[mine, :] = keep[which]
        out[theirs, :] = got[which]


def pair_rows(chip):
    firsts = [2 * ((chip & 1) ^ far) for far in (1, 0)]
    return [(which, first, row, slice(row * TOK, (row + 1) * TOK)) for which, first in enumerate(firsts) for row in (0, 1)]


def window(ext_ref, chip):
    head = jnp.minimum(chip, 2)
    reach_t, reach_h, reach_w = ext_ref[head, 0], ext_ref[head, 1], ext_ref[head, 2]
    s = lax.axis_index("seq")
    y, c = lax.div(s, 8), lax.rem(s, 2)
    near = reach_t >= 1
    outside = ((y == 0) & (c == 0)) | ((y == 3) & (c == 1))
    return (True, near, near & jnp.logical_not(outside)), reach_h, reach_w >= 1


def span_bias(block_ok, reach_h, wide, key_h, first_h):
    lane = lax.broadcasted_iota(jnp.int32, (1, TOK), 1)
    left = lane < TOK // 2
    top, low = [], []
    for j in range(3):
        ok = jnp.abs(first_h + j - key_h) <= reach_h
        if block_ok is not True:
            ok = ok & block_ok
        same = jnp.where(ok, 0.0, -jnp.inf).astype(F32)
        cross = jnp.where(ok & wide, 0.0, -jnp.inf).astype(F32)
        top.append(jnp.where(left, same, cross))
        low.append(jnp.where(left, cross, same))
    return jnp.concatenate(top, 1), jnp.concatenate(low, 1)


def first_height(key_h):
    return jnp.clip(key_h - 1, 0, 1)


def fold(x, how):
    return how(x.reshape(x.shape[0] // 8, 8, x.shape[1]), 0)


def stats_kernel(
    ext_ref, m_far, m_near, core_kv, time_kv, tk_ref, tv_ref, tb_ref,
    lse_ref, mean_ref,
    kb, vb, qb, sb, st, run,
):
    chip = work_chip()
    msgs = (m_far, m_near)
    for which, first, row, part in pair_rows(chip):
        h = first + row
        qb[pl.ds(pl.multiple_of(h * TOK, TOK), TOK), :] = msgs[which][0, part]
        kb[h], vb[h] = msgs[which][1, part], msgs[which][2, part]
        kb[4 + h], vb[4 + h] = core_kv[which, 0, part], core_kv[which, 1, part]
        kb[8 + h], vb[8 + h] = time_kv[which, 0, part], time_kv[which, 1, part]
    block_ok, reach_h, wide = window(ext_ref, chip)
    head = jnp.minimum(chip, 2)
    columns = pl.ds(pl.multiple_of(head * DH, DH), DH)
    factor = INV_ROOT * LOG2E

    text = dot_nt(tk_ref[:, columns], qb[...]) * factor + tb_ref[...]
    st[...] = text
    run[...] = fold(text, jnp.max)

    for part in range(3):

        def first(key_h, carry, part=part):
            h0 = first_height(key_h)
            rows = pl.ds(pl.multiple_of(h0 * TOK, TOK), SPAN)
            top, low = span_bias(block_ok[part], reach_h, wide, key_h, h0)
            s = dot_nt(kb[part * 4 + key_h], qb[rows, :]) * factor
            a, b = s[: TOK // 2] + top, s[TOK // 2 :] + low
            sb[part * 4 + key_h, : TOK // 2] = a
            sb[part * 4 + key_h, TOK // 2 :] = b
            run[:, rows] = jnp.maximum(run[:, rows], jnp.maximum(fold(a, jnp.max), fold(b, jnp.max)))
            return carry

        lax.fori_loop(0, 4, first, 0, unroll=True)

    top_score = jnp.max(run[...], 0, keepdims=True)
    lse_ref[...] = top_score
    weights = jnp.exp2(st[...] - top_score)
    run[...] = fold(weights, jnp.sum)
    mean_ref[...] = dot_tn(tv_ref[:, columns], weights.astype(BF16))

    def second(block, carry):
        key_h = lax.rem(block, 4)
        rows = pl.ds(pl.multiple_of(first_height(key_h) * TOK, TOK), SPAN)
        weights = jnp.exp2(sb[block] - lse_ref[:, rows])
        run[:, rows] += fold(weights, jnp.sum)
        mean_ref[:, rows] += dot_tn(vb[block], weights.astype(BF16))
        return carry

    lax.fori_loop(0, 12, second, 0, unroll=4)
    total = jnp.sum(run[...], 0, keepdims=True)
    lse_ref[...] = top_score + jnp.log2(total)
    mean_ref[...] = mean_ref[...] / total


def block_terms(keys, values, query, grad, bias, delta, factor):
    s = dot_nt(keys, query) * factor
    if isinstance(bias, tuple):
        top, low = bias
        half = TOK // 2
        probs = jnp.concatenate([jnp.exp2(s[:half] + top), jnp.exp2(s[half:] + low)], 0)
    else:
        probs = jnp.exp2(s + bias)
    dprobs = dot_nt(values, grad)
    dscores = (probs * (dprobs - delta)).astype(BF16)
    return probs.astype(BF16), dscores


def place_rows(chip, far_rows, near_rows, out):
    for far, rows in ((1, far_rows), (0, near_rows)):
        first = 2 * ((chip & 1) ^ far)
        out[pl.ds(pl.multiple_of(first * TOK, 2 * TOK), 2 * TOK), :] = rows


def part_grads(part, m_refs, kv_ref, ext_ref, lse_ref, delta_ref, out_ref, dq_ref, kb, vb, qb, gb):
    chip = work_chip()
    for which, first, row, rows in pair_rows(chip):
        kb[first + row] = m_refs[which][1, rows] if part == 0 else kv_ref[which, 0, rows]
        vb[first + row] = m_refs[which][2, rows] if part == 0 else kv_ref[which, 1, rows]
    block_ok, reach_h, wide = window(ext_ref, chip)
    factor = INV_ROOT * LOG2E

    def body(key_h, carry):
        h0 = first_height(key_h)
        rows = pl.ds(pl.multiple_of(h0 * TOK, TOK), SPAN)
        top, low = span_bias(block_ok[part], reach_h, wide, key_h, h0)
        lse = lse_ref[:, rows]
        query, grad, keys = qb[rows, :], gb[rows, :], kb[key_h]
        probs, dscores = block_terms(
            keys, vb[key_h], query, grad, (top - lse, low - lse), delta_ref[:, rows], factor
        )
        out_ref[key_h, 0] = (dot_nn(dscores, query) * INV_ROOT).astype(out_ref.dtype)
        out_ref[key_h, 1] = dot_nn(probs, grad).astype(out_ref.dtype)
        dq_ref[:, rows] += dot_tn(keys, dscores)
        return carry

    lax.fori_loop(0, 4, body, 0, unroll=True)


def time_grads_kernel(
    ext_ref, m_far, m_near, g_far, g_near, time_kv, lse_ref, mean_ref, tk_ref, tv_ref, tb_ref,
    time_out, text_ref, dq_ref, delta_ref, gb,
    kb, vb, qb,
):
    chip = work_chip()
    m_refs = (m_far, m_near)
    place_rows(chip, m_far[0], m_near[0], qb)
    place_rows(chip, g_far[...], g_near[...], gb)
    delta_ref[...] = jnp.sum(gb[...].astype(F32).T * mean_ref[...], 0, keepdims=True)
    head = jnp.minimum(chip, 2)
    columns = pl.ds(pl.multiple_of(head * DH, DH), DH)
    keys = tk_ref[:, columns]
    probs, dscores = block_terms(
        keys, tv_ref[:, columns], qb[...], gb[...], tb_ref[...] - lse_ref[...], delta_ref[...],
        INV_ROOT * LOG2E,
    )
    dq_ref[...] = dot_tn(keys, dscores)
    text_ref[:, :DH] = (dot_nn(dscores, qb[...]) * INV_ROOT).astype(BF16)
    text_ref[:, DH:] = dot_nn(probs, gb[...]).astype(BF16)
    part_grads(2, m_refs, time_kv, ext_ref, lse_ref, delta_ref, time_out, dq_ref, kb, vb, qb, gb)


def near_grads_kernel(
    ext_ref, m_far, m_near, core_kv, lse_ref, dq_in, delta_ref, gb,
    core_out, own_out,
    kb, vb, qb, dq_run,
):
    m_refs = (m_far, m_near)
    place_rows(work_chip(), m_far[0], m_near[0], qb)
    dq_run[...] = dq_in[...]
    part_grads(1, m_refs, core_kv, ext_ref, lse_ref, delta_ref, core_out, dq_run, kb, vb, qb, gb)
    part_grads(0, m_refs, None, ext_ref, lse_ref, delta_ref, own_out, dq_run, kb, vb, qb, gb)
    for h in range(ROWS):
        own_out[h, 2] = dq_run[:, h * TOK : (h + 1) * TOK].T * INV_ROOT


def combine_kernel(own, core, time, text, o0, o1, o2, o3, text_sum):
    chip = work_chip()
    text_sum[...] = jnp.sum(text[...].astype(F32), 0)
    for phase, out in enumerate((o0, o1, o2, o3)):
        h = received_height(phase, chip)
        out[:TOK] = own[h, 2].astype(BF16)
        for which in range(2):
            total = own[h, which] + core[h, which].astype(F32) + time[h, which].astype(F32)
            out[(1 + which) * TOK : (2 + which) * TOK] = total.astype(BF16)
        share = text_sum[pl.ds(pl.multiple_of(h * 8, 8), 8), :]
        out[3 * TOK :] = jnp.concatenate([share[:, :DH], share[:, DH:]], 0).astype(BF16)


def unpack_kernel(r0, r1, r2, r3, dq, dk, dv, tk, tv, buf):
    h = home_height()
    for phase, src in enumerate((r0, r1, r2, r3)):
        buf[sent_head(phase, h)] = src[...]
    for head in range(3):
        columns = slice(head * DH, (head + 1) * DH)
        dq[:, columns] = buf[head, :TOK]
        dk[:, columns] = buf[head, TOK : 2 * TOK].astype(F32)
        dv[:, columns] = buf[head, 2 * TOK : 3 * TOK].astype(F32)
        share = buf[head, 3 * TOK :].astype(F32)
        tk[:, columns] = share[:8]
        tv[:, columns] = share[8:]


def per_device(queries, keys, values, layer_grad, out_weight, text_keys, text_values, extents, text_mask):
    text_bias = jnp.where(text_mask == 1, 0.0, -jnp.inf).astype(F32)[:, None]

    beside = lax.ppermute(layer_grad, "head", head_pairs(0, 1))
    chunks = [
        src if dx == 0 else lax.ppermute(src, "head", head_pairs(dx, 0))
        for src in (layer_grad, beside)
        for dx in range(4)
    ]
    both = [(s, s ^ 1) for s in range(32)]
    inputs = (queries, keys, values)
    packed = pl.pallas_call(
        pack_kernel,
        in_specs=[ANY] * 3 + [VMEM] * 3,
        out_specs=[VMEM] * 2,
        out_shape=[sds((3, 2 * TOK, DH), BF16)] * 2,
        scratch_shapes=[pltpu.VMEM((TOK, 3 * DH), BF16)] * 3 + [pltpu.SemaphoreType.DMA((3,))],
        compiler_params=params(60),
        name="pack_heads",
    )(*inputs, *(lax.ppermute(one, "seq", both) for one in inputs))
    packed = list(packed)
    msgs = [lax.ppermute(one, "seq", pair_pairs(which)) for which, one in zip((1, 0), packed)]
    partial = pl.pallas_call(
        project_first_kernel,
        in_specs=[VMEM] * 5,
        out_specs=VMEM,
        out_shape=sds((4, TOK, DH), F32),
        compiler_params=params(),
        name="project_first",
    )(*chunks[:4], out_weight)
    keep, give = pl.pallas_call(
        project_kernel,
        in_specs=[VMEM] * 6,
        out_specs=[VMEM] * 2,
        out_shape=[sds((2, TOK, DH), BF16)] * 2,
        compiler_params=params(),
        name="project",
    )(*chunks[4:], out_weight, partial)
    got = lax.ppermute(give, "seq", both)
    msgs, got = lax.optimization_barrier((msgs, got))
    kv = jnp.stack([one[1:] for one in msgs])
    core_kv = lax.ppermute(kv, "seq", core_pairs())
    time_kv = lax.ppermute(kv, "seq", time_pairs())

    near, far = pl.pallas_call(
        assemble_kernel,
        in_specs=[VMEM] * 2,
        out_specs=[VMEM] * 2,
        out_shape=[sds((2 * TOK, DH), BF16)] * 2,
        compiler_params=params(),
        name="assemble",
    )(keep, got)
    grads = [lax.ppermute(one, "seq", pair_pairs(which)) for which, one in ((1, far), (0, near))]

    lse, mean = pl.pallas_call(
        stats_kernel,
        in_specs=[SMEM] + [VMEM] * 7,
        out_specs=[VMEM] * 2,
        out_shape=[sds((1, QALL), F32), sds((DH, QALL), F32)],
        scratch_shapes=[
            pltpu.VMEM((12, TOK, DH), BF16),
            pltpu.VMEM((12, TOK, DH), BF16),
            pltpu.VMEM((QALL, DH), BF16),
            pltpu.VMEM((12, TOK, SPAN), F32),
            pltpu.VMEM((TEXT, QALL), F32),
            pltpu.VMEM((8, QALL), F32),
        ],
        compiler_params=params(24),
        cost_estimate=pl.CostEstimate(flops=1000, bytes_accessed=1000, transcendentals=0),
        name="softmax_stats",
    )(extents, *msgs, core_kv, time_kv, text_keys, text_values, text_bias)

    half_sum = sds((4, 2, TOK, DH), BF16)
    scratch = [
        pltpu.VMEM((4, TOK, DH), BF16),
        pltpu.VMEM((4, TOK, DH), BF16),
        pltpu.VMEM((QALL, DH), BF16),
    ]
    cost = pl.CostEstimate(flops=1000, bytes_accessed=1000, transcendentals=0)
    time_part, text_part, dq, delta, grad_rows = pl.pallas_call(
        time_grads_kernel,
        in_specs=[SMEM] + [VMEM] * 10,
        out_specs=[VMEM] * 5,
        out_shape=[
            half_sum,
            sds((TEXT, 2 * DH), BF16),
            sds((DH, QALL), F32),
            sds((1, QALL), F32),
            sds((QALL, DH), BF16),
        ],
        scratch_shapes=scratch,
        compiler_params=params(),
        cost_estimate=cost,
        name="far_grads",
    )(extents, *msgs, *grads, time_kv, lse, mean, text_keys, text_values, text_bias)
    time_back = lax.ppermute(time_part, "seq", time_pairs())
    core_part, own_part = pl.pallas_call(
        near_grads_kernel,
        in_specs=[SMEM] + [VMEM] * 7,
        out_specs=[VMEM] * 2,
        out_shape=[half_sum, sds((4, 3, TOK, DH), F32)],
        scratch_shapes=scratch + [pltpu.VMEM((DH, QALL), F32)],
        compiler_params=params(16),
        cost_estimate=cost,
        name="own_grads",
    )(extents, *msgs, core_kv, lse, dq, delta, grad_rows)
    text_part, own_part = lax.optimization_barrier((text_part, own_part))
    core_back = lax.ppermute(core_part, "seq", core_pairs())
    groups = [[y * 8 + z_hi * 2 + c for y in range(4) for c in range(2)] for z_hi in range(4)]
    text_back = lax.all_to_all(
        text_part.reshape(8, TEXT // 8, 2 * DH), "seq", 0, 0, axis_index_groups=groups
    )

    results = pl.pallas_call(
        combine_kernel,
        in_specs=[VMEM] * 4,
        out_specs=[VMEM] * 4,
        out_shape=[sds((MSG, DH), BF16)] * 4,
        scratch_shapes=[pltpu.VMEM((TEXT // 8, 2 * DH), F32)],
        compiler_params=params(),
        name="combine",
    )(own_part, core_back, time_back, text_back)
    results = [lax.ppermute(one, "seq", back_pairs(phase)) for phase, one in enumerate(results)]

    width = 3 * DH
    return pl.pallas_call(
        unpack_kernel,
        in_specs=[VMEM] * 4,
        out_specs=[VMEM] * 5,
        out_shape=[
            sds((TOK, width), BF16),
            sds((TOK, width), F32),
            sds((TOK, width), F32),
            sds((8, width), F32),
            sds((8, width), F32),
        ],
        scratch_shapes=[pltpu.VMEM((4, MSG, DH), BF16)],
        compiler_params=params(),
        name="unpack",
    )(*results)


def solution(mesh):
    return jax.shard_map(
        per_device,
        mesh=mesh,
        in_specs=(
            P("seq", "head"),
            P("seq", "head"),
            P("seq", "head"),
            P("seq", "head"),
            P("head", None),
            P(None, "head"),
            P(None, "head"),
            P("head", None),
            P(),
        ),
        out_specs=(P("seq", "head"),) * 5,
        check_vma=False,
    )
```
